128 devices in a mesh: py: 8 (over x, y_lo), pz: 16 (over z, y_hi, core).
Axes of the slice: x: 4, y: 4 (y_hi: 2, y_lo: 2; y = y_hi * 2 + y_lo), z: 4, core: 2. Of those that a mesh axis runs over, the one named last changes fastest.
Arguments:
- adjoint: bfloat16 [5, 256, 512, 512], P(None, 'pz', 'py'), may hold values from -6 to 6
- state: bfloat16 [5, 256, 512, 512], P(None, 'pz', 'py'), may hold values from -1.5 to 4, as said below
- metric: bfloat16 [3, 256, 512, 512], P(None, 'pz', 'py'), may hold values from 0.5 to 2
- deriv_x: bfloat16 [512, 512], replicated, may hold values from -0.25 to 0.25
- deriv_y: bfloat16 [512, 512], replicated, may hold values from -0.25 to 0.25
- deriv_z: bfloat16 [256, 256], replicated, may hold values from -0.375 to 0.375
- surf_cells: int32 [512, 128], P(('py', 'pz')), may hold values from 0 to 524287, as said below
- surf_normal: bfloat16 [512, 3, 128], P(('py', 'pz')), may hold values from -5 to 5
- shape_basis: bfloat16 [65536, 256], P(('py', 'pz')), may hold values from -16 to 16
Outputs:
- adjoint_out: bfloat16 [5, 256, 512, 512], P(None, 'pz', 'py')
- shape_grad: float32 [256], replicated
The draws below stay inside these ranges and needn't reach their ends.
Inputs may be any that keep to these rules, and one draw needn't show every extreme that they name: `surf_cells`: each entry of rows r * 4 to (r + 1) * 4 - 1 is z_in * 64 * 512 + y_in * 512 + x for a cell of tile r as the steps define it. `state`: field 0 (density) lies in 0.6 to 1.6 and field 4 (energy) in 2 to 4.
All inputs are finite; a program needn't handle non-finite values.
Results may differ from the reference program's by a relative error of at most 0.0055.
Values may be sent and summed in bfloat16 or wider, within the bound.
No kernel may reach another device: no remote copies, remote signals or barrier semaphores. Data moves between devices by JAX's collectives and lax.ppermute only.
A program may use at most 320 MiB of HBM per device.

```python
import math
import jax
import jax.numpy as jnp
from jax import lax

NX = 512
NY = 512
NZ = 256
DESIGN = 256
SROW_DEV = 4
CY = 64
CZ = 16
LOCAL = 524288
ROWS = 512
SURF = 65536
N_PZ = 16


def draw_state(key, part):
    key = jax.random.fold_in(key, 11)
    subkeys = jax.random.split(key, 3)
    plane_shape = (1, NZ, NY, NX)
    density = jax.random.uniform(subkeys[0], plane_shape, jnp.float32, 0.6, 1.6)
    momenta = jnp.clip(0.5 * jax.random.normal(subkeys[1], (3, NZ, NY, NX), jnp.float32), -1.5, 1.5)
    energy = jax.random.uniform(subkeys[2], plane_shape, jnp.float32, 2.0, 4.0)
    return jnp.concatenate([density, momenta, energy], axis=0).astype(jnp.bfloat16)


def draw_surf_cells(key, part):
    key = jax.random.fold_in(key, 12)
    picked = jax.random.randint(key, (ROWS, 128), 0, LOCAL, dtype=jnp.int32)
    flat_pos = jnp.arange(ROWS * 128, dtype=jnp.int32).reshape(ROWS, 128)
    picked = jnp.where(flat_pos == 0, LOCAL - 1, picked)
    return jnp.where(flat_pos == 1, 0, picked).astype(jnp.int32)


def draw_shape_basis(key, part):
    key = jax.random.fold_in(key, 13)
    subkeys = jax.random.split(key, 2)
    tile_pos = (jnp.arange(SURF) // (SROW_DEV * 128)).astype(jnp.float32) / max(ROWS // SROW_DEV - 1, 1)
    column_scale = jnp.exp(jax.random.uniform(subkeys[1], (1, DESIGN), jnp.float32, 0.0, 2.3026))
    entries = jnp.clip(jax.random.normal(subkeys[0], (SURF, DESIGN), jnp.float32), -4.0, 4.0)
    rising = 1.0 + 2.0 * tile_pos
    return (0.1 * entries * rising[:, None] * column_scale).astype(jnp.bfloat16)


def shard_levels(rng, shape, cuts, low, largest):
    loudness, own = 1.0, jax.random.fold_in(rng, 6)
    for position, shards_of in cuts:
        steps = jnp.exp(jax.random.uniform(jax.random.fold_in(own, position), (shards_of,), jnp.float32, low / len(cuts), largest / len(cuts)))
        loudness = loudness * jnp.repeat(steps, shape[position] // shards_of).reshape([-1 if axis == position else 1 for axis in range(len(shape))])
    return loudness


def scatter_about(key, shape, deviation, reach, cuts=(), kind=jnp.bfloat16):
    gain = shard_levels(key, shape, cuts, -0.22, 0.18) if cuts else 1.0
    values = jax.random.normal(key, shape, jnp.float32) * deviation * gain
    return jnp.minimum(jnp.maximum(values, -reach), reach).astype(kind)


def setup_inputs(seed: int = 0) -> dict:
    arg_keys = jax.random.split(jax.random.key(seed), 10)
    adjoint = scatter_about(arg_keys[0], (5, NZ, NY, NX), 1.0, 6.0, ((1, 16), (2, 8)))
    state = draw_state(jax.random.fold_in(arg_keys[9], 71), 0)
    metric = jnp.clip(jnp.exp(math.log(2.0) - 1.3862944 * jax.random.uniform(arg_keys[2], (3, NZ, NY, NX), jnp.float32) ** shard_levels(arg_keys[2], (3, NZ, NY, NX), ((1, 16), (2, 8)), -0.2, 0.2)), 0.5, 2.0).astype(jnp.bfloat16)
    deriv_x = scatter_about(arg_keys[3], (NX, NX), NX ** -0.5, 0.25)
    deriv_y = scatter_about(arg_keys[4], (NY, NY), NY ** -0.5, 0.25)
    deriv_z = scatter_about(arg_keys[5], (NZ, NZ), NZ ** -0.5, 0.375)
    surf_cells = draw_surf_cells(jax.random.fold_in(arg_keys[9], 71), 0)
    surf_normal = scatter_about(arg_keys[7], (ROWS, 3, 128), 1.0, 5.0, ((0, 128),))
    shape_basis = draw_shape_basis(jax.random.fold_in(arg_keys[9], 71), 0)
    return dict(adjoint=adjoint, state=state, metric=metric, deriv_x=deriv_x, deriv_y=deriv_y, deriv_z=deriv_z, surf_cells=surf_cells, surf_normal=surf_normal, shape_basis=shape_basis)


gamma_less = 0.4
section_step = 0.5

def pressure_of(conserved):
    momenta = conserved[1:4]
    return gamma_less * (conserved[4] - 0.5 * lax.optimization_barrier(jnp.sum(momenta * (momenta / conserved[0]), axis=0)))

def flux_all(conserved):
    density = conserved[0]
    momenta = conserved[1:4]
    energy = conserved[4]
    velocity = momenta / density
    pressure = pressure_of(conserved)
    fluxes = []
    for direction in range(3):
        components = [momenta[direction]]
        for member in range(3):
            summand = momenta[member] * velocity[direction]
            if member == direction:
                summand = summand + pressure
            components.append(summand)
        components.append((energy + pressure) * velocity[direction])
        fluxes.append(jnp.stack(components))
    return jnp.stack(fluxes)

def reference(adjoint, state, metric, deriv_x, deriv_y, deriv_z, surf_cells, surf_normal, shape_basis):
    zblock = 16
    dx_wide = deriv_x.astype(jnp.float32)
    dy_wide = deriv_y.astype(jnp.float32)
    dz_wide = deriv_z.astype(jnp.float32)
    flat_adjoint = adjoint.reshape(5, NZ, NY * NX).astype(jnp.float32)

    def one_block(start):
        lam_block = lax.dynamic_slice_in_dim(adjoint, start, zblock, 1).astype(jnp.float32)
        along_x = jnp.einsum('fzyx,xk->fzyk', lam_block, dx_wide)
        along_y = jnp.einsum('yk,fzyx->fzkx', dy_wide, lam_block).astype(jnp.bfloat16)
        along_y = lax.optimization_barrier(along_y).astype(jnp.float32)
        columns = lax.dynamic_slice_in_dim(dz_wide, start, zblock, 1)
        along_z = jnp.einsum('zk,fzn->fkn', columns, flat_adjoint).astype(jnp.bfloat16)
        along_z = lax.optimization_barrier(along_z).astype(jnp.float32).reshape(5, zblock, NY, NX)
        metric_block = lax.dynamic_slice_in_dim(metric, start, zblock, 1).astype(jnp.float32)
        cotangent = metric_block[:, None] * jnp.stack([along_x, along_y, along_z])
        state_block = lax.dynamic_slice_in_dim(state, start, zblock, 1).astype(jnp.float32)
        unused, pullback = jax.vjp(flux_all, state_block)
        pulled, = pullback(cotangent)
        return (lam_block - section_step * pulled).astype(jnp.bfloat16)
    starts = (jnp.arange(NZ // zblock) * zblock).astype(jnp.int32)
    blocks = lax.map(one_block, starts)
    adjoint_out = jnp.transpose(blocks, (1, 0, 2, 3, 4)).reshape(5, NZ, NY, NX)
    tile = (jnp.arange(ROWS) // SROW_DEV).astype(jnp.int32)
    tile_y = tile // N_PZ
    tile_z = tile % N_PZ
    plane = surf_cells // (CY * NX)
    within = surf_cells % (CY * NX)
    glob_y = tile_y[:, None] * CY + within // NX
    glob_z = tile_z[:, None] * CZ + plane
    flat_cell = ((glob_z * NY + glob_y) * NX + within % NX).astype(jnp.int32)
    picked_out = adjoint_out.reshape(5, -1)[:, flat_cell].astype(jnp.float32)
    picked_state = state.reshape(5, -1)[:, flat_cell].astype(jnp.float32)
    normals = jnp.transpose(surf_normal, (1, 0, 2)).astype(jnp.float32)
    sensitivity = (pressure_of(picked_state) * lax.optimization_barrier(jnp.sum(normals * picked_out[1:4], axis=0))).astype(jnp.bfloat16)
    summed_grad = jnp.dot(sensitivity.reshape(1, -1), shape_basis, preferred_element_type=jnp.float32)[0]
    shape_grad = summed_grad / jnp.sqrt(jnp.mean(summed_grad * summed_grad) + 1e-06)
    return (adjoint_out, shape_grad)
```

```python
import jax
import jax.numpy as jnp
from jax import lax
from jax.experimental import pallas as pl
from jax.experimental.pallas import tpu as pltpu
from jax.sharding import PartitionSpec as P

gamma_less = 0.4
section_step = 0.5
FIELDS, CZ, CY, NX, NZ = 5, 16, 64, 512, 256
CELLS = 512
BF, F32 = jnp.bfloat16, jnp.float32
VMEM_LIMIT = 48 * 1024 * 1024


def params():
    return pltpu.CompilerParams(vmem_limit_bytes=VMEM_LIMIT)


def cost(flops, nbytes):
    return pl.CostEstimate(flops=int(flops), bytes_accessed=int(nbytes), transcendentals=0)


def line_y_kernel(in_ref, op_ref, out_ref):
    line = in_ref[...].reshape(512, NX)
    out = jnp.dot(op_ref[...], line, preferred_element_type=F32)
    out_ref[...] = out.astype(BF).reshape(out_ref.shape)


def line_y(lines, deriv_t):
    n, f, z = lines.shape[:3]
    spec = pl.BlockSpec((n, 1, 1, CY, NX), lambda i, j: (0, i, j, 0, 0))
    return pl.pallas_call(
        line_y_kernel,
        grid=(f, z),
        in_specs=[spec, pl.BlockSpec((512, 512), lambda i, j: (0, 0))],
        out_specs=spec,
        out_shape=jax.ShapeDtypeStruct(lines.shape, BF),
        compiler_params=params(),
        cost_estimate=cost(2 * lines.size * 512, 4 * lines.size),
        name="line_y",
    )(lines, deriv_t)


def line_z_kernel(in_ref, op_ref, *rest):
    outs, (wide, prod) = rest[:-2], rest[-2:]
    wide[...] = in_ref[...].reshape(NZ * 16, 128).astype(F32)
    for row in range(0, 16, 2):
        pair = [wide[pl.ds(row + i, NZ, stride=16), :].astype(BF) for i in range(2)]
        out = jnp.dot(op_ref[...], jnp.concatenate(pair, axis=1), preferred_element_type=F32)
        for i in range(2):
            prod[pl.ds(row + i, NZ, stride=16), :] = out[:, 128 * i : 128 * (i + 1)]
    whole = prod[...].astype(BF).reshape(16, CZ, 16, 128)
    depth = CZ // len(outs)
    for i, out_ref in enumerate(outs):
        out_ref[...] = whole[:, i * depth : (i + 1) * depth].reshape(out_ref.shape)


def line_z(lines, deriv_t, parts):
    f = lines.shape[1]
    depth = CZ // parts
    return pl.pallas_call(
        line_z_kernel,
        grid=(f,),
        in_specs=[
            pl.BlockSpec((16, 1, CZ, 16, 128), lambda i: (0, i, 0, 0, 0)),
            pl.BlockSpec((NZ, NZ), lambda i: (0, 0)),
        ],
        out_specs=[pl.BlockSpec((16, 1, depth, 16, 128), lambda i: (0, i, 0, 0, 0))] * parts,
        out_shape=[jax.ShapeDtypeStruct((16, f, depth, 16, 128), BF)] * parts,
        scratch_shapes=[pltpu.VMEM((NZ * 16, 128), F32), pltpu.VMEM((NZ * 16, 128), F32)],
        compiler_params=params(),
        cost_estimate=cost(2 * lines.size * NZ, 4 * lines.size),
        name="line_z",
    )(lines, deriv_t)


def update(adj, state, metric, alongs):
    recip = 1.0 / state[0]
    vel = [state[1 + i] * recip for i in range(3)]
    speed_sq = vel[0] * vel[0] + vel[1] * vel[1] + vel[2] * vel[2]
    kinetic = 0.5 * (state[1] * vel[0] + state[2] * vel[1] + state[3] * vel[2])
    enthalpy = (state[4] + gamma_less * (state[4] - kinetic)) * recip
    press = energy = back = None
    mom = [None] * 3
    turn = [None] * 3
    plus = lambda a, b: b if a is None else a + b
    for d in range(3):
        weight, along = metric[d], alongs[d]
        weighted_vel = weight * vel[d]
        turn[d] = weight * (
            along[4] * enthalpy + along[1] * vel[0] + along[2] * vel[1] + along[3] * vel[2]
        )
        back = plus(back, turn[d] * vel[d])
        mom[d] = plus(mom[d], weight * along[0])
        for m in range(3):
            mom[m] = plus(mom[m], weighted_vel * along[1 + m])
        work = weighted_vel * along[4]
        energy = plus(energy, work)
        press = plus(press, weight * along[1 + d] + work)
    press = gamma_less * press
    pulled = [0.5 * speed_sq * press - back]
    pulled += [mom[m] + turn[m] - vel[m] * press for m in range(3)]
    pulled += [energy + press]
    return [adj[f] - section_step * pulled[f] for f in range(5)]


def update_kernel(adj_ref, state_ref, metric_ref, op_ref, y_ref, z_ref, *rest):
    out_ref, along_x = rest[-2:]
    along_x[...] = jnp.dot(
        adj_ref[...].reshape(FIELDS * CY, NX), op_ref[...], preferred_element_type=F32
    ).reshape(FIELDS, CY, NX)

    def body(a, carry):
        rows = pl.ds(pl.multiple_of(a * 16, 16), 16)
        for b in range(4):
            cols = slice(128 * b, 128 * b + 128)
            adj = [adj_ref[f, 0, rows, cols].astype(F32) for f in range(5)]
            state = [state_ref[f, 0, rows, cols].astype(F32) for f in range(5)]
            metric = [metric_ref[d, 0, rows, cols].astype(F32) for d in range(3)]
            alongs = [
                [along_x[f, rows, cols] for f in range(5)],
                [y_ref[0, f, 0, rows, cols].astype(F32) for f in range(5)],
                [z_ref[a * 4 + b, f, 0].astype(F32) for f in range(5)],
            ]
            new = update(adj, state, metric, alongs)
            for f in range(5):
                out_ref[f, 0, rows, cols] = new[f].astype(BF)
        return carry

    lax.fori_loop(0, 4, body, 0)


def update_part(adjoint, state, metric, deriv_x, along_y, along_z, first, old):
    depth = along_z.shape[2]
    plane = lambda n: pl.BlockSpec((n, 1, CY, NX), lambda i: (0, i + first, 0, 0))
    in_specs = [
        plane(5),
        plane(5),
        plane(3),
        pl.BlockSpec((NX, NX), lambda i: (0, 0)),
        pl.BlockSpec((1, 5, 1, CY, NX), lambda i: ((i + first) // 2, 0, (i + first) % 2, 0, 0)),
        pl.BlockSpec((16, 5, 1, 16, 128), lambda i: (0, 0, i, 0, 0)),
    ]
    operands = [adjoint, state, metric, deriv_x, along_y, along_z]
    aliases = {}
    if old is not None:
        in_specs.append(pl.BlockSpec(memory_space=pl.ANY))
        aliases = {len(operands): 0}
        operands.append(old)
    cells = depth * CY * NX
    return pl.pallas_call(
        update_kernel,
        grid=(depth,),
        in_specs=in_specs,
        out_specs=plane(5),
        out_shape=jax.ShapeDtypeStruct(adjoint.shape, BF),
        scratch_shapes=[pltpu.VMEM((FIELDS, CY, NX), F32)],
        input_output_aliases=aliases,
        compiler_params=params(),
        cost_estimate=cost(cells * 2 * 5 * NX + cells * 2000, cells * 56),
        name="update",
    )(*operands)


def pick(field, onehot, x_of):
    rows = jnp.dot(onehot, field, preferred_element_type=F32)
    lane = lax.broadcasted_iota(jnp.int32, (CELLS, NX), 1)
    return jnp.sum(jnp.where(lane == x_of, rows, 0.0), axis=1, keepdims=True)


def pick_kernel(cell_ref, field_ref, out_ref, onehot):
    f = pl.program_id(0)
    cell = cell_ref[:, 0:1]

    @pl.when(f == 0)
    def _():
        row = lax.broadcasted_iota(jnp.int32, (CELLS, CZ * CY), 1)
        onehot[...] = (row == cell // NX).astype(F32).astype(BF)

    value = pick(field_ref[...].reshape(CZ * CY, NX), onehot[...], cell % NX)
    lane = lax.broadcasted_iota(jnp.int32, (CELLS, 128), 1)
    old = jnp.where(f == 0, 0.0, out_ref[...])
    out_ref[...] = jnp.where(lane == f, value, old)


def pick_cells(cells, fields, first, count):
    return pl.pallas_call(
        pick_kernel,
        grid=(count,),
        in_specs=[
            pl.BlockSpec((CELLS, 128), lambda f: (0, 0)),
            pl.BlockSpec((1, CZ, CY, NX), lambda f: (f + first, 0, 0, 0)),
        ],
        out_specs=pl.BlockSpec((CELLS, 128), lambda f: (0, 0)),
        out_shape=jax.ShapeDtypeStruct((CELLS, 128), F32),
        scratch_shapes=[pltpu.VMEM((CELLS, CZ * CY), BF)],
        compiler_params=params(),
        cost_estimate=cost(2 * count * CELLS * CZ * CY * NX, count * CZ * CY * NX * 2),
        name="pick_cells",
    )(cells, fields)


def gradient_kernel(picked_ref, state_ref, normal_ref, basis_ref, out_ref):
    state = [state_ref[:, f : f + 1] for f in range(5)]
    work = sum(state[1 + i] * (state[1 + i] / state[0]) for i in range(3))
    press = gamma_less * (state[4] - 0.5 * work)
    force = sum(normal_ref[:, i : i + 1] * picked_ref[:, i : i + 1] for i in range(3))
    sens = (press * force).astype(BF).astype(F32)
    out_ref[...] = jnp.sum(sens * basis_ref[...].astype(F32), axis=0, keepdims=True)


def gradient_terms(picked, state, normals, basis):
    return pl.pallas_call(
        gradient_kernel,
        out_shape=jax.ShapeDtypeStruct((1, 256), F32),
        compiler_params=params(),
        cost_estimate=cost(4 * basis.size, 2 * basis.size),
        name="gradient_terms",
    )(picked, state, normals, basis)


def shift(value, dx=0, yl=0, dz=0, yh=0, core=0):
    pairs = []
    for device in range(128):
        py, pz = divmod(device, 16)
        x, y_lo = divmod(py, 2)
        z, rest = divmod(pz, 4)
        y_hi, c = divmod(rest, 2)
        to_py = (x + dx) % 4 * 2 + (y_lo ^ yl)
        to_pz = (z + dz) % 4 * 4 + (y_hi ^ yh) * 2 + (c ^ core)
        pairs.append((device, to_py * 16 + to_pz))
    return lax.ppermute(value, ("py", "pz"), pairs)


def sum_devices(value):
    for step in ({"core": 1}, {"yl": 1}, {"yh": 1}):
        value = value + shift(value, **step)
    for axis in ("dx", "dz"):
        one, two, three = [shift(value, **{axis: n}) for n in (1, 2, 3)]
        value = (value + two) + (one + three)
    return value


def on_device(
    adjoint, state, metric, deriv_x, deriv_y, deriv_z, surf_cells, surf_normal, shape_basis
):
    to_y = jnp.transpose(adjoint.reshape(5, 8, 2, CY, NX), (1, 0, 2, 3, 4))
    lines_y = lax.all_to_all(to_y, "py", 0, 0)
    to_z = jnp.transpose(adjoint.reshape(5, CZ, 4, 16, 4, 128), (2, 4, 0, 1, 3, 5))
    lines_z = lax.all_to_all(to_z.reshape(16, 5, CZ, 16, 128), "pz", 0, 0)
    back_y = lax.all_to_all(line_y(lines_y, deriv_y.T), "py", 0, 0)
    parts = line_z(lines_z, deriv_z.T, 2)
    back_z = [lax.all_to_all(part, "pz", 0, 0) for part in parts]

    cells = jnp.broadcast_to(surf_cells.reshape(CELLS, 1), (CELLS, 128))
    normals = jnp.transpose(surf_normal, (0, 2, 1)).reshape(CELLS, 3).astype(F32)
    normals = jnp.pad(normals, ((0, 0), (0, 125)))
    picked_state = pick_cells(cells, state, 0, 5)

    result = None
    for i, part in enumerate(back_z):
        result = update_part(
            adjoint, state, metric, deriv_x, back_y, part, i * CZ // 2, result
        )
    picked_out = pick_cells(cells, result, 1, 3)
    partial_grad = gradient_terms(picked_out, picked_state, normals, shape_basis)
    summed_grad = sum_devices(partial_grad)[0]
    gradient_out = summed_grad / jnp.sqrt(jnp.mean(summed_grad * summed_grad) + 1e-06)
    return (result, gradient_out)


def solution(mesh):
    return jax.shard_map(
        on_device,
        mesh=mesh,
        in_specs=(
            P(None, "pz", "py", None),
            P(None, "pz", "py", None),
            P(None, "pz", "py", None),
            P(),
            P(),
            P(),
            P(("py", "pz"), None),
            P(("py", "pz"), None, None),
            P(("py", "pz"), None),
        ),
        out_specs=(P(None, "pz", "py", None), P()),
        check_vma=False,
    )
```

```python
import jax
import jax.numpy as jnp
from jax import lax
from jax.experimental import pallas as pl
from jax.experimental.pallas import tpu as pltpu
from jax.sharding import PartitionSpec as P

gamma_less = 0.4
section_step = 0.5
FIELDS, CZ, CY, NX, NZ = 5, 16, 64, 512, 256
CELLS = 512
BF, F32 = jnp.bfloat16, jnp.float32
VMEM_LIMIT = 48 * 1024 * 1024


def params():
    return pltpu.CompilerParams(vmem_limit_bytes=VMEM_LIMIT)


def cost(flops, nbytes):
    return pl.CostEstimate(flops=int(flops), bytes_accessed=int(nbytes), transcendentals=0)


def line_y_kernel(in_ref, op_ref, out_ref):
    line = in_ref[...].reshape(512, NX)
    out = jnp.dot(op_ref[...], line, preferred_element_type=F32)
    out_ref[...] = out.astype(BF).reshape(out_ref.shape)


def line_y(lines, deriv_t):
    n, f, z = lines.shape[:3]
    spec = pl.BlockSpec((n, 1, 1, CY, NX), lambda i, j: (0, i, j, 0, 0))
    return pl.pallas_call(
        line_y_kernel,
        grid=(f, z),
        in_specs=[spec, pl.BlockSpec((512, 512), lambda i, j: (0, 0))],
        out_specs=spec,
        out_shape=jax.ShapeDtypeStruct(lines.shape, BF),
        compiler_params=params(),
        cost_estimate=cost(2 * lines.size * 512, 4 * lines.size),
        name="line_y",
    )(lines, deriv_t)


def pieces_kernel(in_ref, y_ref, z_ref):
    y_ref[:, 0] = in_ref[0].reshape(y_ref.shape[0], 2, CY, NX)
    for a in range(4):
        for b in range(4):
            z_ref[4 * a + b, 0] = in_ref[0, :, 16 * a : 16 * a + 16, 128 * b : 128 * b + 128]


def pieces(adjoint):
    depth = 8
    return pl.pallas_call(
        pieces_kernel,
        grid=(FIELDS, CZ // depth),
        in_specs=[pl.BlockSpec((1, depth, CY, NX), lambda f, i: (f, i, 0, 0))],
        out_specs=[
            pl.BlockSpec((depth // 2, 1, 2, CY, NX), lambda f, i: (i, f, 0, 0, 0)),
            pl.BlockSpec((16, 1, depth, 16, 128), lambda f, i: (0, f, i, 0, 0)),
        ],
        out_shape=[
            jax.ShapeDtypeStruct((8, FIELDS, 2, CY, NX), BF),
            jax.ShapeDtypeStruct((16, FIELDS, CZ, 16, 128), BF),
        ],
        compiler_params=params(),
        cost_estimate=cost(adjoint.size, 6 * adjoint.size),
        name="pieces",
    )(adjoint)


def line_z_kernel(in_ref, op_ref, *rest):
    outs, (wide, prod) = rest[:-2], rest[-2:]
    wide[...] = in_ref[...].reshape(NZ * 16, 128).astype(F32)
    for row in range(0, 16, 2):
        pair = [wide[pl.ds(row + i, NZ, stride=16), :].astype(BF) for i in range(2)]
        out = jnp.dot(op_ref[...], jnp.concatenate(pair, axis=1), preferred_element_type=F32)
        for i in range(2):
            prod[pl.ds(row + i, NZ, stride=16), :] = out[:, 128 * i : 128 * (i + 1)]
    whole = prod[...].astype(BF).reshape(16, CZ, 16, 128)
    depth = CZ // len(outs)
    for i, out_ref in enumerate(outs):
        out_ref[...] = whole[:, i * depth : (i + 1) * depth].reshape(out_ref.shape)


def line_z(lines, deriv_t, parts):
    f = lines.shape[1]
    depth = CZ // parts
    return pl.pallas_call(
        line_z_kernel,
        grid=(f,),
        in_specs=[
            pl.BlockSpec((16, 1, CZ, 16, 128), lambda i: (0, i, 0, 0, 0)),
            pl.BlockSpec((NZ, NZ), lambda i: (0, 0)),
        ],
        out_specs=[pl.BlockSpec((16, 1, depth, 16, 128), lambda i: (0, i, 0, 0, 0))] * parts,
        out_shape=[jax.ShapeDtypeStruct((16, f, depth, 16, 128), BF)] * parts,
        scratch_shapes=[pltpu.VMEM((NZ * 16, 128), F32), pltpu.VMEM((NZ * 16, 128), F32)],
        compiler_params=params(),
        cost_estimate=cost(2 * lines.size * NZ, 4 * lines.size),
        name="line_z",
    )(lines, deriv_t)


def update(adj, state, metric, alongs):
    recip = 1.0 / state[0]
    vel = [state[1 + i] * recip for i in range(3)]
    speed_sq = vel[0] * vel[0] + vel[1] * vel[1] + vel[2] * vel[2]
    kinetic = 0.5 * (state[1] * vel[0] + state[2] * vel[1] + state[3] * vel[2])
    enthalpy = (state[4] + gamma_less * (state[4] - kinetic)) * recip
    press = energy = back = None
    mom = [None] * 3
    turn = [None] * 3
    plus = lambda a, b: b if a is None else a + b
    for d in range(3):
        weight, along = metric[d], alongs[d]
        weighted_vel = weight * vel[d]
        turn[d] = weight * (
            along[4] * enthalpy + along[1] * vel[0] + along[2] * vel[1] + along[3] * vel[2]
        )
        back = plus(back, turn[d] * vel[d])
        mom[d] = plus(mom[d], weight * along[0])
        for m in range(3):
            mom[m] = plus(mom[m], weighted_vel * along[1 + m])
        work = weighted_vel * along[4]
        energy = plus(energy, work)
        press = plus(press, weight * along[1 + d] + work)
    press = gamma_less * press
    pulled = [0.5 * speed_sq * press - back]
    pulled += [mom[m] + turn[m] - vel[m] * press for m in range(3)]
    pulled += [energy + press]
    return [adj[f] - section_step * pulled[f] for f in range(5)]


def update_kernel(adj_ref, state_ref, metric_ref, op_ref, y_ref, z_ref, *rest):
    out_ref, along_x = rest[-2:]
    along_x[...] = jnp.dot(
        adj_ref[...].reshape(FIELDS * CY, NX), op_ref[...], preferred_element_type=F32
    ).reshape(FIELDS, CY, NX)

    def body(a, carry):
        rows = pl.ds(pl.multiple_of(a * 16, 16), 16)
        for b in range(4):
            cols = slice(128 * b, 128 * b + 128)
            adj = [adj_ref[f, 0, rows, cols].astype(F32) for f in range(5)]
            state = [state_ref[f, 0, rows, cols].astype(F32) for f in range(5)]
            metric = [metric_ref[d, 0, rows, cols].astype(F32) for d in range(3)]
            alongs = [
                [along_x[f, rows, cols] for f in range(5)],
                [y_ref[0, f, 0, rows, cols].astype(F32) for f in range(5)],
                [z_ref[a * 4 + b, f, 0].astype(F32) for f in range(5)],
            ]
            new = update(adj, state, metric, alongs)
            for f in range(5):
                out_ref[f, 0, rows, cols] = new[f].astype(BF)
        return carry

    lax.fori_loop(0, 4, body, 0)


def update_part(adjoint, state, metric, deriv_x, along_y, along_z, first, depth, old, after):
    plane = lambda n: pl.BlockSpec((n, 1, CY, NX), lambda i: (0, i + first, 0, 0))
    in_specs = [
        plane(5),
        plane(5),
        plane(3),
        pl.BlockSpec((NX, NX), lambda i: (0, 0)),
        pl.BlockSpec((1, 5, 1, CY, NX), lambda i: ((i + first) // 2, 0, (i + first) % 2, 0, 0)),
        pl.BlockSpec((16, 5, 1, 16, 128), lambda i: (0, 0, i + first, 0, 0)),
    ]
    operands = [adjoint, state, metric, deriv_x, along_y, along_z]
    aliases = {}
    if old is not None:
        aliases = {len(operands): 0}
        operands.append(old)
    if after is not None:
        operands.append(after)
    in_specs += [pl.BlockSpec(memory_space=pl.ANY)] * (len(operands) - len(in_specs))
    cells = depth * CY * NX
    return pl.pallas_call(
        update_kernel,
        grid=(depth,),
        in_specs=in_specs,
        out_specs=plane(5),
        out_shape=jax.ShapeDtypeStruct(adjoint.shape, BF),
        scratch_shapes=[pltpu.VMEM((FIELDS, CY, NX), F32)],
        input_output_aliases=aliases,
        compiler_params=params(),
        cost_estimate=cost(cells * 2 * 5 * NX + cells * 10000, cells * 56),
        name="update",
    )(*operands)


def pick_rows(onehot_ref, row, f):
    @pl.when(f == 0)
    def _():
        count = onehot_ref.shape[1]
        at = lax.broadcasted_iota(jnp.int32, (CELLS, count), 1)
        onehot_ref[...] = jnp.where(at == row, 1.0, 0.0).astype(BF)

    return onehot_ref[...]


def pick_lane(rows, lane):
    at = lax.broadcasted_iota(jnp.int32, rows.shape, 1)
    return jnp.sum(jnp.where(at == lane, rows, 0.0), axis=1, keepdims=True)


def keep(held, value, f):
    lane = lax.broadcasted_iota(jnp.int32, (CELLS, 128), 1)
    held[...] = jnp.where(lane == f, value, held[...])


def pick_kernel(cell_ref, field_ref, out_ref, onehot_ref, held):
    f = pl.program_id(0)
    cell = cell_ref[:, 0:1]
    onehot = pick_rows(onehot_ref, cell // NX, f)

    @pl.when(f == 0)
    def _():
        held[...] = jnp.zeros_like(held)

    rows = jnp.dot(onehot, field_ref[...].reshape(CZ * CY, NX), preferred_element_type=F32)
    keep(held, pick_lane(rows, cell % NX), f)

    @pl.when(f == pl.num_programs(0) - 1)
    def _():
        out_ref[...] = held[...].T[0:8]


def pick_cells(cells, fields, spec, count):
    return pl.pallas_call(
        pick_kernel,
        grid=(count,),
        in_specs=[pl.BlockSpec((CELLS, 128), lambda f: (0, 0)), spec],
        out_specs=pl.BlockSpec((8, CELLS), lambda f: (0, 0)),
        out_shape=jax.ShapeDtypeStruct((8, CELLS), F32),
        scratch_shapes=[pltpu.VMEM((CELLS, CZ * CY), BF), pltpu.VMEM((CELLS, 128), F32)],
        compiler_params=params(),
        cost_estimate=cost(2 * count * CELLS * CZ * CY * NX, count * CZ * CY * NX * 2),
        name="pick_cells",
    )(cells, fields)


def pick_x_kernel(cell_ref, field_ref, op_ref, adj_out, along_out, onehot_ref, column, held, along):
    f = pl.program_id(0)
    cell = cell_ref[:, 0:1]
    x = cell % NX
    onehot = pick_rows(onehot_ref, cell // NX, f)

    @pl.when(f == 0)
    def _():
        at = lax.broadcasted_iota(jnp.int32, (CELLS, NX), 1)
        pick_x = jnp.where(at == x, 1.0, 0.0).astype(BF)
        column[...] = jnp.dot(pick_x, op_ref[...], preferred_element_type=F32)
        held[...] = jnp.zeros_like(held)
        along[...] = jnp.zeros_like(along)

    rows = jnp.dot(onehot, field_ref[...].reshape(CZ * CY, NX), preferred_element_type=F32)
    keep(held, pick_lane(rows, x), f)
    keep(along, jnp.sum(rows * column[...], axis=1, keepdims=True), f)

    @pl.when(f == pl.num_programs(0) - 1)
    def _():
        adj_out[...] = held[...].T[0:8]
        along_out[...] = along[...].T[0:8]


def pick_x(cells, adjoint, deriv_t):
    return pl.pallas_call(
        pick_x_kernel,
        grid=(FIELDS,),
        in_specs=[
            pl.BlockSpec((CELLS, 128), lambda f: (0, 0)),
            pl.BlockSpec((1, CZ, CY, NX), lambda f: (f, 0, 0, 0)),
            pl.BlockSpec((NX, NX), lambda f: (0, 0)),
        ],
        out_specs=[pl.BlockSpec((8, CELLS), lambda f: (0, 0))] * 2,
        out_shape=[jax.ShapeDtypeStruct((8, CELLS), F32)] * 2,
        scratch_shapes=[
            pltpu.VMEM((CELLS, CZ * CY), BF),
            pltpu.VMEM((CELLS, NX), F32),
            pltpu.VMEM((CELLS, 128), F32),
            pltpu.VMEM((CELLS, 128), F32),
        ],
        compiler_params=params(),
        cost_estimate=cost(2 * 5 * CELLS * CZ * CY * NX, 5 * CZ * CY * NX * 2),
        name="pick_x",
    )(cells, adjoint, deriv_t)


def surface_kernel(
    cell_ref, z_ref, adj_ref, x_ref, y_ref, state_ref, metric_ref, normal_ref, basis_ref, out_ref,
    onehot_ref, held,
):
    f = pl.program_id(0)
    cell = cell_ref[:, 0:1]
    x, y, z = cell % NX, cell // NX % CY, cell // (NX * CY)
    row = ((y // 16 * 4 + x // 128) * CZ + z) * 16 + y % 16
    onehot = pick_rows(onehot_ref, row, f)

    @pl.when(f == 0)
    def _():
        held[...] = jnp.zeros_like(held)

    rows = jnp.dot(onehot, z_ref[...].reshape(16 * CZ * 16, 128), preferred_element_type=F32)
    keep(held, pick_lane(rows, x % 128), f)

    @pl.when(f == FIELDS - 1)
    def _():
        lines = lambda ref, n: [ref[i : i + 1, :] for i in range(n)]
        picked = held[...].T
        along_z = [picked[i : i + 1, :] for i in range(5)]
        state = lines(state_ref, 5)
        new = update(
            lines(adj_ref, 5), state, lines(metric_ref, 3),
            [lines(x_ref, 5), lines(y_ref, 5), along_z],
        )
        work = sum(state[1 + i] * (state[1 + i] / state[0]) for i in range(3))
        press = gamma_less * (state[4] - 0.5 * work)
        normal = lines(normal_ref, 3)
        force = sum(normal[i] * new[1 + i].astype(BF).astype(F32) for i in range(3))
        sens = jnp.broadcast_to((press * force).astype(BF), (16, CELLS))
        out_ref[...] = jnp.dot(sens, basis_ref[...], preferred_element_type=F32)[0:8]


def surface_terms(cells, along_z, adj, along_x, along_y, state, metric, normals, basis):
    small = pl.BlockSpec((8, CELLS), lambda f: (0, 0))
    return pl.pallas_call(
        surface_kernel,
        grid=(FIELDS,),
        in_specs=[
            pl.BlockSpec((CELLS, 128), lambda f: (0, 0)),
            pl.BlockSpec((16, 1, CZ, 16, 128), lambda f: (0, f, 0, 0, 0)),
            small, small, small, small, small, small,
            pl.BlockSpec((CELLS, 256), lambda f: (0, 0)),
        ],
        out_specs=pl.BlockSpec((8, 256), lambda f: (0, 0)),
        out_shape=jax.ShapeDtypeStruct((8, 256), F32),
        scratch_shapes=[pltpu.VMEM((CELLS, 16 * CZ * 16), BF), pltpu.VMEM((CELLS, 128), F32)],
        compiler_params=params(),
        cost_estimate=cost(2 * 5 * CELLS * CZ * CY * NX, 5 * CZ * CY * NX * 2),
        name="surface_terms",
    )(cells, along_z, adj, along_x, along_y, state, metric, normals, basis)


def on_device(
    adjoint, state, metric, deriv_x, deriv_y, deriv_z, surf_cells, surf_normal, shape_basis
):
    to_y, to_z = pieces(adjoint)
    lines_y = lax.all_to_all(to_y, "py", 0, 0)
    surf_cells, to_z, lines_y = lax.optimization_barrier((surf_cells, to_z, lines_y))
    lines_z = lax.all_to_all(to_z, "pz", 0, 0)
    products_y, lines_z = lax.optimization_barrier((line_y(lines_y, deriv_y.T), lines_z))
    back_y = lax.all_to_all(products_y, "py", 0, 0)
    (products_z,) = line_z(lines_z, deriv_z.T, 1)

    cells = jnp.broadcast_to(surf_cells.reshape(CELLS, 1), (CELLS, 128))
    normals = jnp.transpose(surf_normal, (1, 0, 2)).reshape(3, CELLS).astype(F32)
    normals = jnp.pad(normals, ((0, 5), (0, 0)))
    plain = pl.BlockSpec((1, CZ, CY, NX), lambda f: (f, 0, 0, 0))
    picked_state = pick_cells(cells, state, plain, 5)
    picked_metric = pick_cells(cells, metric, plain, 3)
    picked_adj, picked_x = pick_x(cells, adjoint, deriv_x.T)

    products_z, back_y = lax.optimization_barrier((products_z, back_y))
    back_z = lax.all_to_all(products_z, "pz", 0, 0)
    lines = pl.BlockSpec((8, 1, 2, CY, NX), lambda f: (0, f, 0, 0, 0))
    picked_y = pick_cells(cells, back_y, lines, 5)

    terms = surface_terms(
        cells, back_z, picked_adj, picked_x, picked_y, picked_state, picked_metric, normals,
        shape_basis,
    )[0:1]
    result = update_part(
        adjoint, state, metric, deriv_x, back_y, back_z, 0, CZ, None, terms
    )
    all_terms = lax.all_to_all(jnp.broadcast_to(terms, (128, 1, 256)), ("py", "pz"), 0, 0)
    summed_grad = jnp.sum(all_terms, axis=(0, 1))
    gradient_out = summed_grad / jnp.sqrt(jnp.mean(summed_grad * summed_grad) + 1e-06)
    return (result, gradient_out)


def solution(mesh):
    return jax.shard_map(
        on_device,
        mesh=mesh,
        in_specs=(
            P(None, "pz", "py", None),
            P(None, "pz", "py", None),
            P(None, "pz", "py", None),
            P(),
            P(),
            P(),
            P(("py", "pz"), None),
            P(("py", "pz"), None, None),
            P(("py", "pz"), None),
        ),
        out_specs=(P(None, "pz", "py", None), P()),
        check_vma=False,
    )
```

```python
import jax
import jax.numpy as jnp
from jax import lax
from jax.experimental import pallas as pl
from jax.experimental.pallas import tpu as pltpu
from jax.sharding import PartitionSpec as P

gamma_less = 0.4
section_step = 0.5
FIELDS, CZ, CY, NX, NZ = 5, 16, 64, 512, 256
CELLS = 512
BF, F32 = jnp.bfloat16, jnp.float32
VMEM_LIMIT = 48 * 1024 * 1024


def params():
    return pltpu.CompilerParams(vmem_limit_bytes=VMEM_LIMIT)


def cost(flops, nbytes):
    return pl.CostEstimate(flops=int(flops), bytes_accessed=int(nbytes), transcendentals=0)


def line_y_kernel(in_ref, op_ref, out_ref):
    line = in_ref[...].reshape(512, NX)
    out = jnp.dot(op_ref[...], line, preferred_element_type=F32)
    out_ref[...] = out.astype(BF).reshape(out_ref.shape)


def line_y(lines, deriv_t):
    n, f, z = lines.shape[:3]
    spec = pl.BlockSpec((n, 1, 1, CY, NX), lambda i, j: (0, i, j, 0, 0))
    return pl.pallas_call(
        line_y_kernel,
        grid=(f, z),
        in_specs=[spec, pl.BlockSpec((512, 512), lambda i, j: (0, 0))],
        out_specs=spec,
        out_shape=jax.ShapeDtypeStruct(lines.shape, BF),
        compiler_params=params(),
        cost_estimate=cost(2 * lines.size * 512, 4 * lines.size),
        name="line_y",
    )(lines, deriv_t)


def pieces_kernel(in_ref, y_ref, z_ref):
    y_ref[:, 0] = in_ref[0].reshape(y_ref.shape[0], 2, CY, NX)
    for a in range(4):
        for b in range(4):
            z_ref[4 * a + b, 0] = in_ref[0, :, 16 * a : 16 * a + 16, 128 * b : 128 * b + 128]


def pieces(adjoint):
    depth = 8
    return pl.pallas_call(
        pieces_kernel,
        grid=(FIELDS, CZ // depth),
        in_specs=[pl.BlockSpec((1, depth, CY, NX), lambda f, i: (f, i, 0, 0))],
        out_specs=[
            pl.BlockSpec((depth // 2, 1, 2, CY, NX), lambda f, i: (i, f, 0, 0, 0)),
            pl.BlockSpec((16, 1, depth, 16, 128), lambda f, i: (0, f, i, 0, 0)),
        ],
        out_shape=[
            jax.ShapeDtypeStruct((8, FIELDS, 2, CY, NX), BF),
            jax.ShapeDtypeStruct((16, FIELDS, CZ, 16, 128), BF),
        ],
        compiler_params=params(),
        cost_estimate=cost(adjoint.size, 6 * adjoint.size),
        name="pieces",
    )(adjoint)


def line_z_kernel(in_ref, op_ref, *rest):
    outs, (wide, prod) = rest[:-2], rest[-2:]
    wide[...] = in_ref[...].reshape(NZ * 16, 128).astype(F32)
    for row in range(0, 16, 2):
        pair = [wide[pl.ds(row + i, NZ, stride=16), :].astype(BF) for i in range(2)]
        out = jnp.dot(op_ref[...], jnp.concatenate(pair, axis=1), preferred_element_type=F32)
        for i in range(2):
            prod[pl.ds(row + i, NZ, stride=16), :] = out[:, 128 * i : 128 * (i + 1)]
    whole = prod[...].astype(BF).reshape(16, CZ, 16, 128)
    depth = CZ // len(outs)
    for i, out_ref in enumerate(outs):
        out_ref[...] = whole[:, i * depth : (i + 1) * depth].reshape(out_ref.shape)


def line_z(lines, deriv_t, parts):
    f = lines.shape[1]
    depth = CZ // parts
    return pl.pallas_call(
        line_z_kernel,
        grid=(f,),
        in_specs=[
            pl.BlockSpec((16, 1, CZ, 16, 128), lambda i: (0, i, 0, 0, 0)),
            pl.BlockSpec((NZ, NZ), lambda i: (0, 0)),
        ],
        out_specs=[pl.BlockSpec((16, 1, depth, 16, 128), lambda i: (0, i, 0, 0, 0))] * parts,
        out_shape=[jax.ShapeDtypeStruct((16, f, depth, 16, 128), BF)] * parts,
        scratch_shapes=[pltpu.VMEM((NZ * 16, 128), F32), pltpu.VMEM((NZ * 16, 128), F32)],
        compiler_params=params(),
        cost_estimate=cost(2 * lines.size * NZ, 4 * lines.size),
        name="line_z",
    )(lines, deriv_t)


def update(before, state, metric, alongs, directions=(0, 1, 2)):
    recip = 1.0 / state[0]
    vel = [state[1 + i] * recip for i in range(3)]
    speed_sq = vel[0] * vel[0] + vel[1] * vel[1] + vel[2] * vel[2]
    kinetic = 0.5 * (state[1] * vel[0] + state[2] * vel[1] + state[3] * vel[2])
    enthalpy = (state[4] + gamma_less * (state[4] - kinetic)) * recip
    press = energy = back = None
    mom = [None] * 3
    plus = lambda a, b: b if a is None else a + b
    for d in directions:
        weight, along = metric[d], alongs[d]
        weighted_vel = weight * vel[d]
        turn = weight * (
            along[4] * enthalpy + along[1] * vel[0] + along[2] * vel[1] + along[3] * vel[2]
        )
        back = plus(back, turn * vel[d])
        mom[d] = plus(mom[d], weight * along[0] + turn)
        for m in range(3):
            mom[m] = plus(mom[m], weighted_vel * along[1 + m])
        work = weighted_vel * along[4]
        energy = plus(energy, work)
        press = plus(press, weight * along[1 + d] + work)
    press = gamma_less * press
    pulled = [0.5 * speed_sq * press - back]
    pulled += [mom[m] - vel[m] * press for m in range(3)]
    pulled += [energy + press]
    return [before[f] - section_step * pulled[f] for f in range(5)]


def chunks(body):
    def step(a, carry):
        rows = pl.ds(pl.multiple_of(a * 16, 16), 16)
        for b in range(4):
            body(a * 4 + b, rows, slice(128 * b, 128 * b + 128))
        return carry

    lax.fori_loop(0, 4, step, 0)


def update_xy_kernel(adj_ref, state_ref, metric_ref, op_ref, y_ref, out_ref, along_x):
    along_x[...] = jnp.dot(
        adj_ref[...].reshape(FIELDS * CY, NX), op_ref[...], preferred_element_type=F32
    ).reshape(FIELDS, CY, NX)

    def body(piece, rows, cols):
        load = lambda ref, n: [ref[f, 0, rows, cols].astype(F32) for f in range(n)]
        alongs = [
            [along_x[f, rows, cols] for f in range(5)],
            [y_ref[0, f, 0, rows, cols].astype(F32) for f in range(5)],
        ]
        new = update(load(adj_ref, 5), load(state_ref, 5), load(metric_ref, 2), alongs, (0, 1))
        for f in range(5):
            out_ref[f, 0, rows, cols] = new[f]

    chunks(body)


def update_xy(adjoint, state, metric, deriv_x, along_y):
    plane = lambda n: pl.BlockSpec((n, 1, CY, NX), lambda i: (0, i, 0, 0))
    cells = CZ * CY * NX
    return pl.pallas_call(
        update_xy_kernel,
        grid=(CZ,),
        in_specs=[
            plane(5),
            plane(5),
            plane(2),
            pl.BlockSpec((NX, NX), lambda i: (0, 0)),
            pl.BlockSpec((1, 5, 1, CY, NX), lambda i: (i // 2, 0, i % 2, 0, 0)),
        ],
        out_specs=plane(5),
        out_shape=jax.ShapeDtypeStruct(adjoint.shape, F32),
        scratch_shapes=[pltpu.VMEM((FIELDS, CY, NX), F32)],
        compiler_params=params(),
        cost_estimate=cost(cells * 2 * 5 * NX + cells * 10000, cells * 54),
        name="update_xy",
    )(adjoint, state, metric, deriv_x, along_y)


def update_z_kernel(before_ref, state_ref, metric_ref, z_ref, after_ref, out_ref):
    def body(piece, rows, cols):
        before = [before_ref[f, 0, rows, cols] for f in range(5)]
        state = [state_ref[f, 0, rows, cols].astype(F32) for f in range(5)]
        metric = {2: metric_ref[0, 0, rows, cols].astype(F32)}
        along = {2: [z_ref[piece, f, 0].astype(F32) for f in range(5)]}
        new = update(before, state, metric, along, (2,))
        for f in range(5):
            out_ref[f, 0, rows, cols] = new[f].astype(BF)

    chunks(body)


def update_z(before, state, metric, along_z, after):
    plane = lambda n: pl.BlockSpec((n, 1, CY, NX), lambda i: (0, i, 0, 0))
    cells = CZ * CY * NX
    return pl.pallas_call(
        update_z_kernel,
        grid=(CZ,),
        in_specs=[
            plane(5),
            plane(5),
            pl.BlockSpec((1, 1, CY, NX), lambda i: (2, i, 0, 0)),
            pl.BlockSpec((16, 5, 1, 16, 128), lambda i: (0, 0, i, 0, 0)),
            pl.BlockSpec(memory_space=pl.ANY),
        ],
        out_specs=plane(5),
        out_shape=jax.ShapeDtypeStruct(state.shape, BF),
        compiler_params=params(),
        cost_estimate=cost(cells * 10000, cells * 52),
        name="update_z",
    )(before, state, metric, along_z, after)


def pick_rows(onehot_ref, row, f):
    @pl.when(f == 0)
    def _():
        count = onehot_ref.shape[1]
        at = lax.broadcasted_iota(jnp.int32, (CELLS, count), 1)
        onehot_ref[...] = jnp.where(at == row, 1.0, 0.0).astype(BF)

    return onehot_ref[...]


def pick_lane(rows, lane):
    at = lax.broadcasted_iota(jnp.int32, rows.shape, 1)
    return jnp.sum(jnp.where(at == lane, rows, 0.0), axis=1, keepdims=True)


def keep(held, value, f):
    lane = lax.broadcasted_iota(jnp.int32, (CELLS, 128), 1)
    held[...] = jnp.where(lane == f, value, held[...])


def pick_kernel(cell_ref, field_ref, out_ref, onehot_ref, held):
    f = pl.program_id(0)
    cell = cell_ref[:, 0:1]
    onehot = pick_rows(onehot_ref, cell // NX, f)

    @pl.when(f == 0)
    def _():
        held[...] = jnp.zeros_like(held)

    rows = jnp.dot(onehot, field_ref[...].reshape(CZ * CY, NX), preferred_element_type=F32)
    keep(held, pick_lane(rows, cell % NX), f)

    @pl.when(f == pl.num_programs(0) - 1)
    def _():
        out_ref[...] = held[...].T[0:8]


def pick_cells(cells, fields, spec, count):
    return pl.pallas_call(
        pick_kernel,
        grid=(count,),
        in_specs=[pl.BlockSpec((CELLS, 128), lambda f: (0, 0)), spec],
        out_specs=pl.BlockSpec((8, CELLS), lambda f: (0, 0)),
        out_shape=jax.ShapeDtypeStruct((8, CELLS), F32),
        scratch_shapes=[pltpu.VMEM((CELLS, CZ * CY), BF), pltpu.VMEM((CELLS, 128), F32)],
        compiler_params=params(),
        cost_estimate=cost(2 * count * CELLS * CZ * CY * NX, count * CZ * CY * NX * 2),
        name="pick_cells",
    )(cells, fields)


def pick_x_kernel(cell_ref, field_ref, op_ref, adj_out, along_out, onehot_ref, column, held, along):
    f = pl.program_id(0)
    cell = cell_ref[:, 0:1]
    x = cell % NX
    onehot = pick_rows(onehot_ref, cell // NX, f)

    @pl.when(f == 0)
    def _():
        at = lax.broadcasted_iota(jnp.int32, (CELLS, NX), 1)
        pick_x = jnp.where(at == x, 1.0, 0.0).astype(BF)
        column[...] = jnp.dot(pick_x, op_ref[...], preferred_element_type=F32)
        held[...] = jnp.zeros_like(held)
        along[...] = jnp.zeros_like(along)

    rows = jnp.dot(onehot, field_ref[...].reshape(CZ * CY, NX), preferred_element_type=F32)
    keep(held, pick_lane(rows, x), f)
    keep(along, jnp.sum(rows * column[...], axis=1, keepdims=True), f)

    @pl.when(f == pl.num_programs(0) - 1)
    def _():
        adj_out[...] = held[...].T[0:8]
        along_out[...] = along[...].T[0:8]


def pick_x(cells, adjoint, deriv_t):
    return pl.pallas_call(
        pick_x_kernel,
        grid=(FIELDS,),
        in_specs=[
            pl.BlockSpec((CELLS, 128), lambda f: (0, 0)),
            pl.BlockSpec((1, CZ, CY, NX), lambda f: (f, 0, 0, 0)),
            pl.BlockSpec((NX, NX), lambda f: (0, 0)),
        ],
        out_specs=[pl.BlockSpec((8, CELLS), lambda f: (0, 0))] * 2,
        out_shape=[jax.ShapeDtypeStruct((8, CELLS), F32)] * 2,
        scratch_shapes=[
            pltpu.VMEM((CELLS, CZ * CY), BF),
            pltpu.VMEM((CELLS, NX), F32),
            pltpu.VMEM((CELLS, 128), F32),
            pltpu.VMEM((CELLS, 128), F32),
        ],
        compiler_params=params(),
        cost_estimate=cost(2 * 5 * CELLS * CZ * CY * NX, 5 * CZ * CY * NX * 2),
        name="pick_x",
    )(cells, adjoint, deriv_t)


def rows_z_kernel(cell_ref, out_ref):
    cell = cell_ref[:, 0:1]
    x, y, z = cell % NX, cell // NX % CY, cell // (NX * CY)
    row = ((y // 16 * 4 + x // 128) * CZ + z) * 16 + y % 16 - pl.program_id(0) * 1024
    at = lax.broadcasted_iota(jnp.int32, (CELLS, 1024), 1)
    out_ref[...] = jnp.where(at == row, 1.0, 0.0).astype(BF)


def rows_z(cells):
    return pl.pallas_call(
        rows_z_kernel,
        grid=(4,),
        in_specs=[pl.BlockSpec((CELLS, 128), lambda i: (0, 0))],
        out_specs=pl.BlockSpec((CELLS, 1024), lambda i: (0, i)),
        out_shape=jax.ShapeDtypeStruct((CELLS, 4096), BF),
        compiler_params=params(),
        cost_estimate=cost(CELLS * 4096 * 10, CELLS * 4096 * 2),
        name="rows_z",
    )(cells)


def surface_kernel(
    cell_ref, onehot_ref, z_ref, adj_ref, x_ref, y_ref, state_ref, metric_ref, normal_ref,
    basis_ref, out_ref, total,
):
    step = pl.program_id(0)

    @pl.when(step == 0)
    def _():
        total[...] = jnp.zeros_like(total)

    fields = [z_ref[:, f].reshape(1024, 128) for f in range(FIELDS)]
    total[...] += jnp.dot(
        onehot_ref[...], jnp.concatenate(fields, axis=1), preferred_element_type=F32
    )

    @pl.when(step == pl.num_programs(0) - 1)
    def _():
        lane = lax.broadcasted_iota(jnp.int32, (CELLS, 128), 1)
        here = lane == cell_ref[:, 0:1] % 128
        held = jnp.zeros((CELLS, 128), F32)
        for f in range(FIELDS):
            value = jnp.where(here, total[:, 128 * f : 128 * (f + 1)], 0.0)
            held = jnp.where(lane == f, jnp.sum(value, axis=1, keepdims=True), held)
        lines = lambda ref, n: [ref[i : i + 1, :] for i in range(n)]
        picked = held.T
        along_z = [picked[i : i + 1, :] for i in range(5)]
        state = lines(state_ref, 5)
        new = update(
            lines(adj_ref, 5), state, lines(metric_ref, 3),
            [lines(x_ref, 5), lines(y_ref, 5), along_z],
        )
        work = sum(state[1 + i] * (state[1 + i] / state[0]) for i in range(3))
        press = gamma_less * (state[4] - 0.5 * work)
        normal = lines(normal_ref, 3)
        force = sum(normal[i] * new[1 + i].astype(BF).astype(F32) for i in range(3))
        sens = jnp.broadcast_to((press * force).astype(BF), (16, CELLS))
        out_ref[...] = jnp.dot(sens, basis_ref[...], preferred_element_type=F32)[0:8]


def surface_terms(cells, onehot, along_z, adj, along_x, along_y, state, metric, normals, basis):
    small = pl.BlockSpec((8, CELLS), lambda i: (0, 0))
    return pl.pallas_call(
        surface_kernel,
        grid=(4,),
        in_specs=[
            pl.BlockSpec((CELLS, 128), lambda i: (0, 0)),
            pl.BlockSpec((CELLS, 1024), lambda i: (0, i)),
            pl.BlockSpec((4, FIELDS, CZ, 16, 128), lambda i: (i, 0, 0, 0, 0)),
            small, small, small, small, small, small,
            pl.BlockSpec((CELLS, 256), lambda i: (0, 0)),
        ],
        out_specs=pl.BlockSpec((8, 256), lambda i: (0, 0)),
        out_shape=jax.ShapeDtypeStruct((8, 256), F32),
        scratch_shapes=[pltpu.VMEM((CELLS, FIELDS * 128), F32)],
        compiler_params=params(),
        cost_estimate=cost(2 * 5 * CELLS * CZ * CY * NX, 5 * CZ * CY * NX * 2),
        name="surface_terms",
    )(cells, onehot, along_z, adj, along_x, along_y, state, metric, normals, basis)


def on_device(
    adjoint, state, metric, deriv_x, deriv_y, deriv_z, surf_cells, surf_normal, shape_basis
):
    to_y, to_z = pieces(adjoint)
    lines_y = lax.all_to_all(to_y, "py", 0, 0)
    surf_cells, to_z, lines_y = lax.optimization_barrier((surf_cells, to_z, lines_y))
    lines_z = lax.all_to_all(to_z, "pz", 0, 0)
    products_y, lines_z = lax.optimization_barrier((line_y(lines_y, deriv_y.T), lines_z))
    back_y = lax.all_to_all(products_y, "py", 0, 0)
    (products_z,) = line_z(lines_z, deriv_z.T, 1)

    cells = jnp.broadcast_to(surf_cells.reshape(CELLS, 1), (CELLS, 128))
    normals = jnp.transpose(surf_normal, (1, 0, 2)).reshape(3, CELLS).astype(F32)
    normals = jnp.pad(normals, ((0, 5), (0, 0)))
    plain = pl.BlockSpec((1, CZ, CY, NX), lambda f: (f, 0, 0, 0))
    picked_state = pick_cells(cells, state, plain, 5)
    picked_metric = pick_cells(cells, metric, plain, 3)
    picked_adj, picked_x = pick_x(cells, adjoint, deriv_x.T)

    products_z, back_y = lax.optimization_barrier((products_z, back_y))
    back_z = lax.all_to_all(products_z, "pz", 0, 0)
    lines = pl.BlockSpec((8, 1, 2, CY, NX), lambda f: (0, f, 0, 0, 0))
    picked_y = pick_cells(cells, back_y, lines, 5)
    before = update_xy(adjoint, state, metric, deriv_x, back_y)

    back_z, before, onehot, picked_y = lax.optimization_barrier(
        (back_z, before, rows_z(cells), picked_y)
    )
    terms = surface_terms(
        cells, onehot, back_z, picked_adj, picked_x, picked_y, picked_state,
        picked_metric, normals, shape_basis,
    )[0:1]
    result = update_z(before, state, metric, back_z, terms)
    all_terms = lax.all_to_all(jnp.broadcast_to(terms, (128, 1, 256)), ("py", "pz"), 0, 0)
    summed_grad = jnp.sum(all_terms, axis=(0, 1))
    gradient_out = summed_grad / jnp.sqrt(jnp.mean(summed_grad * summed_grad) + 1e-06)
    return (result, gradient_out)


def solution(mesh):
    return jax.shard_map(
        on_device,
        mesh=mesh,
        in_specs=(
            P(None, "pz", "py", None),
            P(None, "pz", "py", None),
            P(None, "pz", "py", None),
            P(),
            P(),
            P(),
            P(("py", "pz"), None),
            P(("py", "pz"), None, None),
            P(("py", "pz"), None),
        ),
        out_specs=(P(None, "pz", "py", None), P()),
        check_vma=False,
    )
```

```python
import jax
import jax.numpy as jnp
from jax import lax
from jax.experimental import pallas as pl
from jax.experimental.pallas import tpu as pltpu
from jax.sharding import PartitionSpec as P

gamma_less = 0.4
section_step = 0.5
FIELDS, CZ, CY, NX, NZ = 5, 16, 64, 512, 256
CELLS = 512
PLANES = 4
BF, F32 = jnp.bfloat16, jnp.float32
MIB = 1024 * 1024


def params(mib=60):
    return pltpu.CompilerParams(vmem_limit_bytes=mib * MIB)


def cost(flops, nbytes):
    return pl.CostEstimate(flops=int(flops), bytes_accessed=int(nbytes), transcendentals=0)


def line_y_kernel(in_ref, op_ref, out_ref):
    line = in_ref[...].reshape(512, NX)
    out = jnp.dot(op_ref[...], line, preferred_element_type=F32)
    out_ref[...] = out.astype(BF).reshape(out_ref.shape)


def line_y(lines, deriv_t):
    n, f, z = lines.shape[:3]
    spec = pl.BlockSpec((n, 1, 1, CY, NX), lambda i, j: (0, i, j, 0, 0))
    return pl.pallas_call(
        line_y_kernel,
        grid=(f, z),
        in_specs=[spec, pl.BlockSpec((512, 512), lambda i, j: (0, 0))],
        out_specs=spec,
        out_shape=jax.ShapeDtypeStruct(lines.shape, BF),
        compiler_params=params(),
        cost_estimate=cost(2 * lines.size * 512, 4 * lines.size),
        name="line_y",
    )(lines, deriv_t)


def pieces_kernel(in_ref, y_ref, z_ref):
    y_ref[:, 0] = in_ref[0].reshape(y_ref.shape[0], 2, CY, NX)
    for a in range(4):
        for b in range(4):
            z_ref[4 * a + b, 0] = in_ref[0, :, 16 * a : 16 * a + 16, 128 * b : 128 * b + 128]


def pieces(adjoint):
    depth = 8
    return pl.pallas_call(
        pieces_kernel,
        grid=(FIELDS, CZ // depth),
        in_specs=[pl.BlockSpec((1, depth, CY, NX), lambda f, i: (f, i, 0, 0))],
        out_specs=[
            pl.BlockSpec((depth // 2, 1, 2, CY, NX), lambda f, i: (i, f, 0, 0, 0)),
            pl.BlockSpec((16, 1, depth, 16, 128), lambda f, i: (0, f, i, 0, 0)),
        ],
        out_shape=[
            jax.ShapeDtypeStruct((8, FIELDS, 2, CY, NX), BF),
            jax.ShapeDtypeStruct((16, FIELDS, CZ, 16, 128), BF),
        ],
        compiler_params=params(8),
        cost_estimate=cost(adjoint.size, 6 * adjoint.size),
        name="pieces",
    )(adjoint)


def line_z_kernel(in_ref, op_ref, out_ref, held, made, in_sem, out_sem):
    fetch, send = [], []
    for f in range(FIELDS):
        fetch.append(pltpu.make_async_copy(in_ref.at[:, f], held.at[f], in_sem.at[f]))
        send.append(pltpu.make_async_copy(made.at[f], out_ref.at[:, f], out_sem.at[f]))
        fetch[f].start()
    for f in range(FIELDS):
        fetch[f].wait()
        line = held[f].reshape(NZ, 16 * 128)
        out = jnp.dot(op_ref[...], line, preferred_element_type=F32).astype(BF)
        made[f] = out.reshape(16, CZ, 16, 128)
        send[f].start()
    for copy in send:
        copy.wait()


def line_z(lines, deriv_t):
    tile = pltpu.VMEM((FIELDS, 16, CZ, 16, 128), BF)
    return pl.pallas_call(
        line_z_kernel,
        in_specs=[pl.BlockSpec(memory_space=pl.ANY), pl.BlockSpec(memory_space=pltpu.VMEM)],
        out_specs=pl.BlockSpec(memory_space=pl.ANY),
        out_shape=jax.ShapeDtypeStruct(lines.shape, BF),
        scratch_shapes=[
            tile,
            tile,
            pltpu.SemaphoreType.DMA((FIELDS,)),
            pltpu.SemaphoreType.DMA((FIELDS,)),
        ],
        compiler_params=params(),
        cost_estimate=cost(2 * lines.size * NZ, 4 * lines.size),
        name="line_z",
    )(lines, deriv_t)


def update(before, state, metric, alongs, directions=(0, 1, 2)):
    recip = 1.0 / state[0]
    vel = [state[1 + i] * recip for i in range(3)]
    speed_sq = vel[0] * vel[0] + vel[1] * vel[1] + vel[2] * vel[2]
    kinetic = 0.5 * (state[1] * vel[0] + state[2] * vel[1] + state[3] * vel[2])
    enthalpy = (state[4] + gamma_less * (state[4] - kinetic)) * recip
    press = energy = back = None
    mom = [None] * 3
    plus = lambda a, b: b if a is None else a + b
    for d in directions:
        weight, along = metric[d], alongs[d]
        weighted_vel = weight * vel[d]
        turn = weight * (
            along[4] * enthalpy + along[1] * vel[0] + along[2] * vel[1] + along[3] * vel[2]
        )
        back = plus(back, turn * vel[d])
        mom[d] = plus(mom[d], weight * along[0] + turn)
        for m in range(3):
            mom[m] = plus(mom[m], weighted_vel * along[1 + m])
        work = weighted_vel * along[4]
        energy = plus(energy, work)
        press = plus(press, weight * along[1 + d] + work)
    press = gamma_less * press
    pulled = [0.5 * speed_sq * press - back]
    pulled += [mom[m] - vel[m] * press for m in range(3)]
    pulled += [energy + press]
    return [before[f] - section_step * pulled[f] for f in range(5)]


def chunks(body):
    def step(n, carry):
        z, a = n // 4, n % 4
        rows = pl.ds(pl.multiple_of(a * 16, 16), 16)
        for b in range(4):
            body(z, a * 4 + b, rows, slice(128 * b, 128 * b + 128))
        return carry

    lax.fori_loop(0, PLANES * 4, step, 0)


def update_xy_kernel(adj_ref, state_ref, metric_ref, op_ref, y_ref, out_ref, along_x):
    for f in range(FIELDS):
        along_x[f] = jnp.dot(
            adj_ref[f].reshape(PLANES * CY, NX), op_ref[...], preferred_element_type=F32
        ).reshape(PLANES, CY, NX)

    def body(z, piece, rows, cols):
        load = lambda ref, n: [ref[f, z, rows, cols].astype(F32) for f in range(n)]
        alongs = [
            [along_x[f, z, rows, cols] for f in range(5)],
            [y_ref[z // 2, f, z % 2, rows, cols].astype(F32) for f in range(5)],
        ]
        new = update(load(adj_ref, 5), load(state_ref, 5), load(metric_ref, 2), alongs, (0, 1))
        for f in range(5):
            out_ref[f, z, rows, cols] = new[f]

    chunks(body)


def update_xy(adjoint, state, metric, deriv_x, along_y):
    plane = lambda n: pl.BlockSpec((n, PLANES, CY, NX), lambda i: (0, i, 0, 0))
    cells = CZ * CY * NX
    return pl.pallas_call(
        update_xy_kernel,
        grid=(CZ // PLANES,),
        in_specs=[
            plane(5),
            plane(5),
            plane(2),
            pl.BlockSpec((NX, NX), lambda i: (0, 0)),
            pl.BlockSpec((PLANES // 2, 5, 2, CY, NX), lambda i: (i, 0, 0, 0, 0)),
        ],
        out_specs=plane(5),
        out_shape=jax.ShapeDtypeStruct(adjoint.shape, F32),
        scratch_shapes=[pltpu.VMEM((FIELDS, PLANES, CY, NX), F32)],
        compiler_params=params(),
        cost_estimate=cost(cells * 2 * 5 * NX + cells * 10000, cells * 54),
        name="update_xy",
    )(adjoint, state, metric, deriv_x, along_y)


def update_z_kernel(before_ref, state_ref, metric_ref, z_ref, after_ref, out_ref):
    def body(z, piece, rows, cols):
        before = [before_ref[f, z, rows, cols] for f in range(5)]
        state = [state_ref[f, z, rows, cols].astype(F32) for f in range(5)]
        metric = {2: metric_ref[0, z, rows, cols].astype(F32)}
        along = {2: [z_ref[piece, f, z].astype(F32) for f in range(5)]}
        new = update(before, state, metric, along, (2,))
        for f in range(5):
            out_ref[f, z, rows, cols] = new[f].astype(BF)

    chunks(body)


def update_z(before, state, metric, along_z, after):
    plane = lambda n: pl.BlockSpec((n, PLANES, CY, NX), lambda i: (0, i, 0, 0))
    cells = CZ * CY * NX
    return pl.pallas_call(
        update_z_kernel,
        grid=(CZ // PLANES,),
        in_specs=[
            plane(5),
            plane(5),
            pl.BlockSpec((1, PLANES, CY, NX), lambda i: (2, i, 0, 0)),
            pl.BlockSpec((16, 5, PLANES, 16, 128), lambda i: (0, 0, i, 0, 0)),
            pl.BlockSpec(memory_space=pl.ANY),
        ],
        out_specs=plane(5),
        out_shape=jax.ShapeDtypeStruct(state.shape, BF),
        compiler_params=params(),
        cost_estimate=cost(cells * 10000, cells * 52),
        name="update_z",
    )(before, state, metric, along_z, after)


def pick_rows(onehot_ref, row, f):
    @pl.when(f == 0)
    def _():
        count = onehot_ref.shape[1]
        at = lax.broadcasted_iota(jnp.int32, (CELLS, count), 1)
        onehot_ref[...] = jnp.where(at == row, 1.0, 0.0).astype(BF)

    return onehot_ref[...]


def pick_lane(rows, lane):
    at = lax.broadcasted_iota(jnp.int32, rows.shape, 1)
    return jnp.sum(jnp.where(at == lane, rows, 0.0), axis=1, keepdims=True)


def keep(held, value, f):
    lane = lax.broadcasted_iota(jnp.int32, (CELLS, 128), 1)
    held[...] = jnp.where(lane == f, value, held[...])


def pick_kernel(cell_ref, field_ref, out_ref, onehot_ref, held):
    f = pl.program_id(0)
    cell = cell_ref[:, 0:1]
    onehot = pick_rows(onehot_ref, cell // NX, f)

    @pl.when(f == 0)
    def _():
        held[...] = jnp.zeros_like(held)

    rows = jnp.dot(onehot, field_ref[...].reshape(CZ * CY, NX), preferred_element_type=F32)
    keep(held, pick_lane(rows, cell % NX), f)

    @pl.when(f == pl.num_programs(0) - 1)
    def _():
        out_ref[...] = held[...].T[0:8]


def pick_cells(cells, fields, spec, count):
    return pl.pallas_call(
        pick_kernel,
        grid=(count,),
        in_specs=[pl.BlockSpec((CELLS, 128), lambda f: (0, 0)), spec],
        out_specs=pl.BlockSpec((8, CELLS), lambda f: (0, 0)),
        out_shape=jax.ShapeDtypeStruct((8, CELLS), F32),
        scratch_shapes=[pltpu.VMEM((CELLS, CZ * CY), BF), pltpu.VMEM((CELLS, 128), F32)],
        compiler_params=params(),
        cost_estimate=cost(2 * count * CELLS * CZ * CY * NX, count * CZ * CY * NX * 2),
        name="pick_cells",
    )(cells, fields)


def pick_x_kernel(cell_ref, field_ref, op_ref, adj_out, along_out, onehot_ref, column, held, along):
    f = pl.program_id(0)
    cell = cell_ref[:, 0:1]
    x = cell % NX
    onehot = pick_rows(onehot_ref, cell // NX, f)

    @pl.when(f == 0)
    def _():
        at = lax.broadcasted_iota(jnp.int32, (CELLS, NX), 1)
        pick_x = jnp.where(at == x, 1.0, 0.0).astype(BF)
        column[...] = jnp.dot(pick_x, op_ref[...], preferred_element_type=F32)
        held[...] = jnp.zeros_like(held)
        along[...] = jnp.zeros_like(along)

    rows = jnp.dot(onehot, field_ref[...].reshape(CZ * CY, NX), preferred_element_type=F32)
    keep(held, pick_lane(rows, x), f)
    keep(along, jnp.sum(rows * column[...], axis=1, keepdims=True), f)

    @pl.when(f == pl.num_programs(0) - 1)
    def _():
        adj_out[...] = held[...].T[0:8]
        along_out[...] = along[...].T[0:8]


def pick_x(cells, adjoint, deriv_t):
    return pl.pallas_call(
        pick_x_kernel,
        grid=(FIELDS,),
        in_specs=[
            pl.BlockSpec((CELLS, 128), lambda f: (0, 0)),
            pl.BlockSpec((1, CZ, CY, NX), lambda f: (f, 0, 0, 0)),
            pl.BlockSpec((NX, NX), lambda f: (0, 0)),
        ],
        out_specs=[pl.BlockSpec((8, CELLS), lambda f: (0, 0))] * 2,
        out_shape=[jax.ShapeDtypeStruct((8, CELLS), F32)] * 2,
        scratch_shapes=[
            pltpu.VMEM((CELLS, CZ * CY), BF),
            pltpu.VMEM((CELLS, NX), F32),
            pltpu.VMEM((CELLS, 128), F32),
            pltpu.VMEM((CELLS, 128), F32),
        ],
        compiler_params=params(),
        cost_estimate=cost(2 * 5 * CELLS * CZ * CY * NX, 5 * CZ * CY * NX * 2),
        name="pick_x",
    )(cells, adjoint, deriv_t)


def surface_kernel(
    cell_ref, z_ref, adj_ref, x_ref, y_ref, state_ref, metric_ref, normal_ref, basis_ref,
    out_ref, pieces_z, sem,
):
    fetch = []
    for n in range(4):
        part = pl.ds(4 * n, 4)
        fetch.append(pltpu.make_async_copy(z_ref.at[part], pieces_z.at[part], sem.at[n]))
        fetch[n].start()
    cell = cell_ref[:, 0:1]
    x, y, z = cell % NX, cell // NX % CY, cell // (NX * CY)
    row = ((y // 16 * 4 + x // 128) * CZ + z) * 16 + y % 16
    total = jnp.zeros((CELLS, FIELDS * 128), F32)
    for n in range(4):
        at = lax.broadcasted_iota(jnp.int32, (CELLS, 1024), 1) + 1024 * n
        onehot = jnp.where(at == row, 1.0, 0.0).astype(BF)
        fetch[n].wait()
        fields = [pieces_z[4 * n : 4 * n + 4, f].reshape(1024, 128) for f in range(FIELDS)]
        total += jnp.dot(
            onehot, jnp.concatenate(fields, axis=1), preferred_element_type=F32
        )
    lane = lax.broadcasted_iota(jnp.int32, (CELLS, 128), 1)
    here = lane == x % 128
    held = jnp.zeros((CELLS, 128), F32)
    for f in range(FIELDS):
        value = jnp.where(here, total[:, 128 * f : 128 * (f + 1)], 0.0)
        held = jnp.where(lane == f, jnp.sum(value, axis=1, keepdims=True), held)
    lines = lambda ref, n: [ref[i : i + 1, :] for i in range(n)]
    picked = held.T
    along_z = [picked[i : i + 1, :] for i in range(5)]
    state = lines(state_ref, 5)
    new = update(
        lines(adj_ref, 5), state, lines(metric_ref, 3),
        [lines(x_ref, 5), lines(y_ref, 5), along_z],
    )
    work = sum(state[1 + i] * (state[1 + i] / state[0]) for i in range(3))
    press = gamma_less * (state[4] - 0.5 * work)
    normal = lines(normal_ref, 3)
    force = sum(normal[i] * new[1 + i].astype(BF).astype(F32) for i in range(3))
    sens = jnp.broadcast_to((press * force).astype(BF), (16, CELLS))
    out_ref[...] = jnp.dot(sens, basis_ref[...], preferred_element_type=F32)[0:8]


def surface_terms(cells, along_z, adj, along_x, along_y, state, metric, normals, basis):
    vmem = pl.BlockSpec(memory_space=pltpu.VMEM)
    return pl.pallas_call(
        surface_kernel,
        in_specs=[vmem, pl.BlockSpec(memory_space=pl.ANY)] + [vmem] * 7,
        out_specs=vmem,
        out_shape=jax.ShapeDtypeStruct((8, 256), F32),
        scratch_shapes=[
            pltpu.VMEM((16, FIELDS, CZ, 16, 128), BF),
            pltpu.SemaphoreType.DMA((4,)),
        ],
        compiler_params=params(),
        cost_estimate=cost(2 * 5 * CELLS * CZ * CY * NX, 5 * CZ * CY * NX * 2),
        name="surface_terms",
    )(cells, along_z, adj, along_x, along_y, state, metric, normals, basis)


def on_device(
    adjoint, state, metric, deriv_x, deriv_y, deriv_z, surf_cells, surf_normal, shape_basis
):
    to_y, to_z = pieces(adjoint)
    lines_y = lax.all_to_all(to_y, "py", 0, 0)

    operators = (deriv_x, deriv_y, deriv_z)
    (deriv_x, deriv_y, deriv_z), surf_cells, surf_normal, to_z, lines_y = lax.optimization_barrier(
        (operators, surf_cells, surf_normal, to_z, lines_y)
    )
    lines_z = lax.all_to_all(to_z, "pz", 0, 0)
    products_y = line_y(lines_y, deriv_y.T)
    cells = jnp.broadcast_to(surf_cells.reshape(CELLS, 1), (CELLS, 128))
    normals = jnp.transpose(surf_normal, (1, 0, 2)).reshape(3, CELLS).astype(F32)
    normals = jnp.pad(normals, ((0, 5), (0, 0)))
    plain = pl.BlockSpec((1, CZ, CY, NX), lambda f: (f, 0, 0, 0))
    picked_state = pick_cells(cells, state, plain, 5)
    picked_metric = pick_cells(cells, metric, plain, 3)
    picked_adj, picked_x = pick_x(cells, adjoint, deriv_x.T)
    picked = (picked_adj, picked_x, picked_state, picked_metric)
    products_y, lines_z, cells, normals, picked, deriv_zt = lax.optimization_barrier(
        (products_y, lines_z, cells, normals, picked, deriv_z.T)
    )
    picked_adj, picked_x, picked_state, picked_metric = picked

    back_y = lax.all_to_all(products_y, "py", 0, 0)
    lines_z, back_y, cells, deriv_x = lax.optimization_barrier((lines_z, back_y, cells, deriv_x))
    back_z = lax.all_to_all(line_z(lines_z, deriv_zt), "pz", 0, 0)

    lines = pl.BlockSpec((8, 1, 2, CY, NX), lambda f: (0, f, 0, 0, 0))
    picked_y = pick_cells(cells, back_y, lines, 5)
    before = update_xy(adjoint, state, metric, deriv_x, back_y)
    back_z, before, picked_y = lax.optimization_barrier((back_z, before, picked_y))
    terms = surface_terms(
        cells, back_z, picked_adj, picked_x, picked_y, picked_state, picked_metric, normals,
        shape_basis,
    )[0:1]
    result = update_z(before, state, metric, back_z, terms)
    all_terms = lax.all_to_all(jnp.broadcast_to(terms, (128, 1, 256)), ("py", "pz"), 0, 0)
    summed_grad = jnp.sum(all_terms, axis=(0, 1))
    gradient_out = summed_grad / jnp.sqrt(jnp.mean(summed_grad * summed_grad) + 1e-06)
    return (result, gradient_out)


def solution(mesh):
    return jax.shard_map(
        on_device,
        mesh=mesh,
        in_specs=(
            P(None, "pz", "py", None),
            P(None, "pz", "py", None),
            P(None, "pz", "py", None),
            P(),
            P(),
            P(),
            P(("py", "pz"), None),
            P(("py", "pz"), None, None),
            P(("py", "pz"), None),
        ),
        out_specs=(P(None, "pz", "py", None), P()),
        check_vma=False,
    )
```

```python
import jax
import jax.numpy as jnp
from jax import lax
from jax.experimental import pallas as pl
from jax.experimental.pallas import tpu as pltpu
from jax.sharding import PartitionSpec as P

gamma_less = 0.4
section_step = 0.5
FIELDS, CZ, CY, NX, NZ = 5, 16, 64, 512, 256
CELLS = 512
PLANES = 4
BF, F32 = jnp.bfloat16, jnp.float32
MIB = 1024 * 1024


def params(mib=24):
    return pltpu.CompilerParams(vmem_limit_bytes=mib * MIB)


def in_hbm(*arrays):
    return [pltpu.with_memory_space_constraint(array, pltpu.HBM) for array in arrays]


def in_vmem(array):
    return pltpu.with_memory_space_constraint(array, pltpu.VMEM)


def hbm_out(shape, dtype):
    return pltpu.HBM(shape, dtype)


def cost(flops, nbytes):
    return pl.CostEstimate(flops=int(flops), bytes_accessed=int(nbytes), transcendentals=0)


def line_y_kernel(in_ref, op_ref, out_ref):
    line = in_ref[...].reshape(512, NX)
    out = jnp.dot(op_ref[...], line, preferred_element_type=F32)
    out_ref[...] = out.astype(BF).reshape(out_ref.shape)


def line_y(lines, deriv_t):
    n, f, z = lines.shape[:3]
    spec = pl.BlockSpec((n, 1, 1, CY, NX), lambda i, j: (0, i, j, 0, 0))
    return pl.pallas_call(
        line_y_kernel,
        grid=(f, z),
        in_specs=[spec, pl.BlockSpec((512, 512), lambda i, j: (0, 0))],
        out_specs=spec,
        out_shape=hbm_out(lines.shape, BF),
        compiler_params=params(),
        cost_estimate=cost(2 * lines.size * 512, 4 * lines.size),
        name="line_y",
    )(*in_hbm(lines), deriv_t)


def pieces_kernel(in_ref, y_ref, z_ref):
    y_ref[:, 0] = in_ref[0].reshape(y_ref.shape[0], 2, CY, NX)
    for a in range(4):
        for b in range(4):
            z_ref[4 * a + b, 0] = in_ref[0, :, 16 * a : 16 * a + 16, 128 * b : 128 * b + 128]


def pieces(adjoint):
    depth = 8
    return pl.pallas_call(
        pieces_kernel,
        grid=(FIELDS, CZ // depth),
        in_specs=[pl.BlockSpec((1, depth, CY, NX), lambda f, i: (f, i, 0, 0))],
        out_specs=[
            pl.BlockSpec((depth // 2, 1, 2, CY, NX), lambda f, i: (i, f, 0, 0, 0)),
            pl.BlockSpec((16, 1, depth, 16, 128), lambda f, i: (0, f, i, 0, 0)),
        ],
        out_shape=[
            jax.ShapeDtypeStruct((8, FIELDS, 2, CY, NX), BF),
            jax.ShapeDtypeStruct((16, FIELDS, CZ, 16, 128), BF),
        ],
        compiler_params=params(8),
        cost_estimate=cost(adjoint.size, 6 * adjoint.size),
        name="pieces",
    )(adjoint)


def line_z_kernel(in_ref, op_ref, out_ref, held, made, in_sem, out_sem):
    fetch, send = [], []
    for f in range(FIELDS):
        fetch.append(pltpu.make_async_copy(in_ref.at[:, f], held.at[f], in_sem.at[f]))
        send.append(pltpu.make_async_copy(made.at[f], out_ref.at[:, f], out_sem.at[f]))
        fetch[f].start()
    for f in range(FIELDS):
        fetch[f].wait()
        line = held[f].reshape(NZ, 16 * 128)
        out = jnp.dot(op_ref[...], line, preferred_element_type=F32).astype(BF)
        made[f] = out.reshape(16, CZ, 16, 128)
        send[f].start()
    for copy in send:
        copy.wait()


def line_z(lines, deriv_t):
    tile = pltpu.VMEM((FIELDS, 16, CZ, 16, 128), BF)
    return pl.pallas_call(
        line_z_kernel,
        in_specs=[pl.BlockSpec(memory_space=pl.ANY), pl.BlockSpec(memory_space=pltpu.VMEM)],
        out_specs=pl.BlockSpec(memory_space=pl.ANY),
        out_shape=hbm_out(lines.shape, BF),
        scratch_shapes=[
            tile,
            tile,
            pltpu.SemaphoreType.DMA((FIELDS,)),
            pltpu.SemaphoreType.DMA((FIELDS,)),
        ],
        compiler_params=params(),
        cost_estimate=cost(2 * lines.size * NZ, 4 * lines.size),
        name="line_z",
    )(in_vmem(lines), deriv_t)


def update(before, state, metric, alongs, directions=(0, 1, 2)):
    recip = 1.0 / state[0]
    vel = [state[1 + i] * recip for i in range(3)]
    speed_sq = vel[0] * vel[0] + vel[1] * vel[1] + vel[2] * vel[2]
    kinetic = 0.5 * (state[1] * vel[0] + state[2] * vel[1] + state[3] * vel[2])
    enthalpy = (state[4] + gamma_less * (state[4] - kinetic)) * recip
    press = energy = back = None
    mom = [None] * 3
    plus = lambda a, b: b if a is None else a + b
    for d in directions:
        weight, along = metric[d], alongs[d]
        weighted_vel = weight * vel[d]
        turn = weight * (
            along[4] * enthalpy + along[1] * vel[0] + along[2] * vel[1] + along[3] * vel[2]
        )
        back = plus(back, turn * vel[d])
        mom[d] = plus(mom[d], weight * along[0] + turn)
        for m in range(3):
            mom[m] = plus(mom[m], weighted_vel * along[1 + m])
        work = weighted_vel * along[4]
        energy = plus(energy, work)
        press = plus(press, weight * along[1 + d] + work)
    press = gamma_less * press
    pulled = [0.5 * speed_sq * press - back]
    pulled += [mom[m] - vel[m] * press for m in range(3)]
    pulled += [energy + press]
    return [before[f] - section_step * pulled[f] for f in range(5)]


def chunks(body):
    def step(n, carry):
        z, a = n // 4, n % 4
        rows = pl.ds(pl.multiple_of(a * 16, 16), 16)
        for b in range(4):
            body(z, a * 4 + b, rows, slice(128 * b, 128 * b + 128))
        return carry

    lax.fori_loop(0, PLANES * 4, step, 0)


def update_xy_kernel(adj_ref, state_ref, metric_ref, op_ref, y_ref, out_ref, along_x):
    for f in range(FIELDS):
        along_x[f] = jnp.dot(
            adj_ref[f].reshape(PLANES * CY, NX), op_ref[...], preferred_element_type=F32
        ).reshape(PLANES, CY, NX)

    def body(z, piece, rows, cols):
        load = lambda ref, n: [ref[f, z, rows, cols].astype(F32) for f in range(n)]
        alongs = [
            [along_x[f, z, rows, cols] for f in range(5)],
            [y_ref[z // 2, f, z % 2, rows, cols].astype(F32) for f in range(5)],
        ]
        new = update(load(adj_ref, 5), load(state_ref, 5), load(metric_ref, 2), alongs, (0, 1))
        for f in range(5):
            out_ref[f, z, rows, cols] = new[f]

    chunks(body)


def update_xy(adjoint, state, metric, deriv_x, along_y):
    plane = lambda n: pl.BlockSpec((n, PLANES, CY, NX), lambda i: (0, i, 0, 0))
    cells = CZ * CY * NX
    return pl.pallas_call(
        update_xy_kernel,
        grid=(CZ // PLANES,),
        in_specs=[
            plane(5),
            plane(5),
            plane(2),
            pl.BlockSpec((NX, NX), lambda i: (0, 0)),
            pl.BlockSpec((PLANES // 2, 5, 2, CY, NX), lambda i: (i, 0, 0, 0, 0)),
        ],
        out_specs=plane(5),
        out_shape=hbm_out(adjoint.shape, F32),
        scratch_shapes=[pltpu.VMEM((FIELDS, PLANES, CY, NX), F32)],
        compiler_params=params(),
        cost_estimate=cost(cells * 2 * 5 * NX + cells * 10000, cells * 54),
        name="update_xy",
    )(*in_hbm(adjoint, state, metric, deriv_x, along_y))


def update_z_kernel(before_ref, state_ref, metric_ref, z_ref, after_ref, out_ref):
    def body(z, piece, rows, cols):
        before = [before_ref[f, z, rows, cols] for f in range(5)]
        state = [state_ref[f, z, rows, cols].astype(F32) for f in range(5)]
        metric = {2: metric_ref[0, z, rows, cols].astype(F32)}
        along = {2: [z_ref[piece, f, z].astype(F32) for f in range(5)]}
        new = update(before, state, metric, along, (2,))
        for f in range(5):
            out_ref[f, z, rows, cols] = new[f].astype(BF)

    chunks(body)


def update_z(before, state, metric, along_z, after):
    plane = lambda n: pl.BlockSpec((n, PLANES, CY, NX), lambda i: (0, i, 0, 0))
    cells = CZ * CY * NX
    return pl.pallas_call(
        update_z_kernel,
        grid=(CZ // PLANES,),
        in_specs=[
            plane(5),
            plane(5),
            pl.BlockSpec((1, PLANES, CY, NX), lambda i: (2, i, 0, 0)),
            pl.BlockSpec((16, 5, PLANES, 16, 128), lambda i: (0, 0, i, 0, 0)),
            pl.BlockSpec(memory_space=pl.ANY),
        ],
        out_specs=plane(5),
        out_shape=jax.ShapeDtypeStruct(state.shape, BF),
        compiler_params=params(),
        cost_estimate=cost(cells * 10000, cells * 52),
        name="update_z",
    )(*in_hbm(before, state, metric), in_vmem(along_z), after)


def pick_rows(onehot_ref, row, f):
    @pl.when(f == 0)
    def _():
        count = onehot_ref.shape[1]
        at = lax.broadcasted_iota(jnp.int32, (CELLS, count), 1)
        onehot_ref[...] = jnp.where(at == row, 1.0, 0.0).astype(BF)

    return onehot_ref[...]


def pick_lane(rows, lane):
    at = lax.broadcasted_iota(jnp.int32, rows.shape, 1)
    return jnp.sum(jnp.where(at == lane, rows, 0.0), axis=1, keepdims=True)


def keep(held, value, f):
    lane = lax.broadcasted_iota(jnp.int32, (CELLS, 128), 1)
    held[...] = jnp.where(lane == f, value, held[...])


def pick_kernel(cell_ref, field_ref, out_ref, onehot_ref, held):
    f = pl.program_id(0)
    cell = cell_ref[:, 0:1]
    onehot = pick_rows(onehot_ref, cell // NX, f)

    @pl.when(f == 0)
    def _():
        held[...] = jnp.zeros_like(held)

    rows = jnp.dot(onehot, field_ref[...].reshape(CZ * CY, NX), preferred_element_type=F32)
    keep(held, pick_lane(rows, cell % NX), f)

    @pl.when(f == pl.num_programs(0) - 1)
    def _():
        out_ref[...] = held[...].T[0:8]


def pick_cells(cells, fields, spec, count):
    return pl.pallas_call(
        pick_kernel,
        grid=(count,),
        in_specs=[pl.BlockSpec((CELLS, 128), lambda f: (0, 0)), spec],
        out_specs=pl.BlockSpec((8, CELLS), lambda f: (0, 0)),
        out_shape=jax.ShapeDtypeStruct((8, CELLS), F32),
        scratch_shapes=[pltpu.VMEM((CELLS, CZ * CY), BF), pltpu.VMEM((CELLS, 128), F32)],
        compiler_params=params(),
        cost_estimate=cost(2 * count * CELLS * CZ * CY * NX, count * CZ * CY * NX * 2),
        name="pick_cells",
    )(cells, *in_hbm(fields))


def pick_x_kernel(cell_ref, field_ref, op_ref, adj_out, along_out, onehot_ref, column, held, along):
    f = pl.program_id(0)
    cell = cell_ref[:, 0:1]
    x = cell % NX
    onehot = pick_rows(onehot_ref, cell // NX, f)

    @pl.when(f == 0)
    def _():
        at = lax.broadcasted_iota(jnp.int32, (CELLS, NX), 1)
        pick_x = jnp.where(at == x, 1.0, 0.0).astype(BF)
        column[...] = jnp.dot(pick_x, op_ref[...], preferred_element_type=F32)
        held[...] = jnp.zeros_like(held)
        along[...] = jnp.zeros_like(along)

    rows = jnp.dot(onehot, field_ref[...].reshape(CZ * CY, NX), preferred_element_type=F32)
    keep(held, pick_lane(rows, x), f)
    keep(along, jnp.sum(rows * column[...], axis=1, keepdims=True), f)

    @pl.when(f == pl.num_programs(0) - 1)
    def _():
        adj_out[...] = held[...].T[0:8]
        along_out[...] = along[...].T[0:8]


def pick_x(cells, adjoint, deriv_t):
    return pl.pallas_call(
        pick_x_kernel,
        grid=(FIELDS,),
        in_specs=[
            pl.BlockSpec((CELLS, 128), lambda f: (0, 0)),
            pl.BlockSpec((1, CZ, CY, NX), lambda f: (f, 0, 0, 0)),
            pl.BlockSpec((NX, NX), lambda f: (0, 0)),
        ],
        out_specs=[pl.BlockSpec((8, CELLS), lambda f: (0, 0))] * 2,
        out_shape=[jax.ShapeDtypeStruct((8, CELLS), F32)] * 2,
        scratch_shapes=[
            pltpu.VMEM((CELLS, CZ * CY), BF),
            pltpu.VMEM((CELLS, NX), F32),
            pltpu.VMEM((CELLS, 128), F32),
            pltpu.VMEM((CELLS, 128), F32),
        ],
        compiler_params=params(),
        cost_estimate=cost(2 * 5 * CELLS * CZ * CY * NX, 5 * CZ * CY * NX * 2),
        name="pick_x",
    )(cells, *in_hbm(adjoint), deriv_t)


def surface_kernel(
    cell_ref, z_ref, adj_ref, x_ref, y_ref, state_ref, metric_ref, normal_ref, basis_ref,
    out_ref, onehot, total,
):
    cell = cell_ref[:, 0:1]
    x, y, z = cell % NX, cell // NX % CY, cell // (NX * CY)
    row = ((y // 16 * 4 + x // 128) * CZ + z) * 16 + y % 16
    for n in range(4):
        at = lax.broadcasted_iota(jnp.int32, (CELLS, 1024), 1) + 1024 * n
        onehot[:, 1024 * n : 1024 * (n + 1)] = jnp.where(at == row, 1.0, 0.0).astype(BF)
    fields = [z_ref[:, f].reshape(4096, 128) for f in range(FIELDS)]
    total[...] = jnp.dot(
        onehot[...], jnp.concatenate(fields, axis=1), preferred_element_type=F32
    )
    lane = lax.broadcasted_iota(jnp.int32, (CELLS, 128), 1)
    here = lane == x % 128
    held = jnp.zeros((CELLS, 128), F32)
    for f in range(FIELDS):
        value = jnp.where(here, total[:, 128 * f : 128 * (f + 1)], 0.0)
        held = jnp.where(lane == f, jnp.sum(value, axis=1, keepdims=True), held)
    lines = lambda ref, n: [ref[i : i + 1, :] for i in range(n)]
    picked = held.T
    along_z = [picked[i : i + 1, :] for i in range(5)]
    state = lines(state_ref, 5)
    new = update(
        lines(adj_ref, 5), state, lines(metric_ref, 3),
        [lines(x_ref, 5), lines(y_ref, 5), along_z],
    )
    work = sum(state[1 + i] * (state[1 + i] / state[0]) for i in range(3))
    press = gamma_less * (state[4] - 0.5 * work)
    normal = lines(normal_ref, 3)
    force = sum(normal[i] * new[1 + i].astype(BF).astype(F32) for i in range(3))
    sens = jnp.broadcast_to((press * force).astype(BF), (16, CELLS))
    terms = jnp.dot(sens, basis_ref[...], preferred_element_type=F32)[0:1]
    out_ref[...] = jnp.broadcast_to(terms.reshape(1, 1, 256), out_ref.shape)


def surface_terms(cells, along_z, adj, along_x, along_y, state, metric, normals, basis):
    vmem = pl.BlockSpec(memory_space=pltpu.VMEM)
    return pl.pallas_call(
        surface_kernel,
        in_specs=[vmem] * 9,
        out_specs=vmem,
        out_shape=jax.ShapeDtypeStruct((128, 1, 256), F32),
        scratch_shapes=[
            pltpu.VMEM((CELLS, 4096), BF),
            pltpu.VMEM((CELLS, FIELDS * 128), F32),
        ],
        compiler_params=params(),
        cost_estimate=cost(2 * 5 * CELLS * CZ * CY * NX, 5 * CZ * CY * NX * 2),
        name="surface_terms",
    )(cells, in_vmem(along_z), adj, along_x, along_y, state, metric, normals, basis)


def normalized_kernel(terms_ref, out_ref):
    summed = jnp.sum(terms_ref[...], axis=0)
    mean = jnp.sum(summed * summed, axis=1, keepdims=True) * (1.0 / 256)
    out_ref[...] = summed / jnp.sqrt(mean + 1e-06)


def normalized(terms):
    return pl.pallas_call(
        normalized_kernel,
        out_shape=jax.ShapeDtypeStruct((1, 256), F32),
        cost_estimate=cost(4 * terms.size, 4 * terms.size),
        name="normalized",
    )(terms)


def on_device(
    adjoint, state, metric, deriv_x, deriv_y, deriv_z, surf_cells, surf_normal, shape_basis
):
    to_y, to_z = pieces(adjoint)
    lines_y = lax.all_to_all(to_y, "py", 0, 0)

    operators = (deriv_x, deriv_y, deriv_z)
    (deriv_x, deriv_y, deriv_z), surf_cells, surf_normal, to_z, lines_y = lax.optimization_barrier(
        (operators, surf_cells, surf_normal, to_z, lines_y)
    )
    lines_z = lax.all_to_all(to_z, "pz", 0, 0)
    products_y = line_y(lines_y, deriv_y.T)
    cells = jnp.broadcast_to(surf_cells.reshape(CELLS, 1), (CELLS, 128))
    normals = jnp.transpose(surf_normal, (1, 0, 2)).reshape(3, CELLS).astype(F32)
    normals = jnp.pad(normals, ((0, 5), (0, 0)))
    plain = pl.BlockSpec((1, CZ, CY, NX), lambda f: (f, 0, 0, 0))
    picked_state = pick_cells(cells, state, plain, 5)
    picked_metric = pick_cells(cells, metric, plain, 3)
    picked_adj, picked_x = pick_x(cells, adjoint, deriv_x.T)
    picked = (picked_adj, picked_x, picked_state, picked_metric)
    products_y, lines_z, cells, normals, picked, deriv_zt = lax.optimization_barrier(
        (products_y, lines_z, cells, normals, picked, deriv_z.T)
    )
    picked_adj, picked_x, picked_state, picked_metric = picked

    back_y = lax.all_to_all(products_y, "py", 0, 0)
    lines_z, back_y, cells, deriv_x = lax.optimization_barrier((lines_z, back_y, cells, deriv_x))
    back_z = lax.all_to_all(line_z(lines_z, deriv_zt), "pz", 0, 0)

    lines = pl.BlockSpec((8, 1, 2, CY, NX), lambda f: (0, f, 0, 0, 0))
    picked_y = pick_cells(cells, back_y, lines, 5)
    before = update_xy(adjoint, state, metric, deriv_x, back_y)
    back_z, before, picked_y = lax.optimization_barrier((back_z, before, picked_y))
    terms = surface_terms(
        cells, back_z, picked_adj, picked_x, picked_y, picked_state, picked_metric, normals,
        shape_basis,
    )
    result = update_z(before, state, metric, back_z, terms)
    all_terms = lax.all_to_all(terms, ("py", "pz"), 0, 0)
    return (result, normalized(all_terms)[0])


def solution(mesh):
    return jax.shard_map(
        on_device,
        mesh=mesh,
        in_specs=(
            P(None, "pz", "py", None),
            P(None, "pz", "py", None),
            P(None, "pz", "py", None),
            P(),
            P(),
            P(),
            P(("py", "pz"), None),
            P(("py", "pz"), None, None),
            P(("py", "pz"), None),
        ),
        out_specs=(P(None, "pz", "py", None), P()),
        check_vma=False,
    )
```

```python
import jax
import jax.numpy as jnp
from jax import lax
from jax.experimental import pallas as pl
from jax.experimental.pallas import tpu as pltpu
from jax.sharding import PartitionSpec as P

gamma_less = 0.4
section_step = 0.5
FIELDS, CZ, CY, NX, NZ = 5, 16, 64, 512, 256
CELLS = 512
PLANES = 4
BF, F32 = jnp.bfloat16, jnp.float32
MIB = 1024 * 1024


def params(mib=24):
    return pltpu.CompilerParams(vmem_limit_bytes=mib * MIB)


def in_hbm(*arrays):
    return [pltpu.with_memory_space_constraint(array, pltpu.HBM) for array in arrays]


def in_vmem(array):
    return pltpu.with_memory_space_constraint(array, pltpu.VMEM)


def hbm_out(shape, dtype):
    return pltpu.HBM(shape, dtype)


def cost(flops, nbytes):
    return pl.CostEstimate(flops=int(flops), bytes_accessed=int(nbytes), transcendentals=0)


def line_y_kernel(in_ref, op_ref, out_ref):
    line = in_ref[...].reshape(512, NX)
    out = jnp.dot(op_ref[...], line, preferred_element_type=F32)
    out_ref[...] = out.astype(BF).reshape(out_ref.shape)


def line_y(lines, deriv_t):
    n, f, z = lines.shape[:3]
    spec = pl.BlockSpec((n, 1, 1, CY, NX), lambda i, j: (0, i, j, 0, 0))
    return pl.pallas_call(
        line_y_kernel,
        grid=(f, z),
        in_specs=[spec, pl.BlockSpec((512, 512), lambda i, j: (0, 0))],
        out_specs=spec,
        out_shape=hbm_out(lines.shape, BF),
        compiler_params=params(),
        cost_estimate=cost(2 * lines.size * 512, 4 * lines.size),
        name="line_y",
    )(*in_hbm(lines), deriv_t)


def pieces_kernel(in_ref, y_ref, z_ref, sem):
    fetch = []
    for f in range(FIELDS):
        for i in range(8):
            planes = in_ref.at[f, pl.ds(2 * i, 2)]
            fetch.append(pltpu.make_async_copy(planes, y_ref.at[i, f], sem.at[8 * f + i]))
            fetch[-1].start()
    for f in range(FIELDS):
        for i in range(8):
            fetch[8 * f + i].wait()
            for a in range(4):
                for b in range(4):
                    part = y_ref[i, f, :, 16 * a : 16 * a + 16, 128 * b : 128 * b + 128]
                    z_ref[4 * a + b, f, 2 * i : 2 * i + 2] = part


def pieces(adjoint):
    vmem = pl.BlockSpec(memory_space=pltpu.VMEM)
    return pl.pallas_call(
        pieces_kernel,
        in_specs=[pl.BlockSpec(memory_space=pl.ANY)],
        out_specs=[vmem, vmem],
        out_shape=[
            pltpu.VMEM((8, FIELDS, 2, CY, NX), BF),
            pltpu.VMEM((16, FIELDS, CZ, 16, 128), BF),
        ],
        scratch_shapes=[pltpu.SemaphoreType.DMA((FIELDS * 8,))],
        compiler_params=params(),
        cost_estimate=cost(adjoint.size, 6 * adjoint.size),
        name="pieces",
    )(*in_hbm(adjoint))


def line_z_kernel(in_ref, op_ref, out_ref, held, made, in_sem, out_sem):
    fetch, send = [], []
    for f in range(FIELDS):
        fetch.append(pltpu.make_async_copy(in_ref.at[:, f], held.at[f], in_sem.at[f]))
        send.append(pltpu.make_async_copy(made.at[f], out_ref.at[:, f], out_sem.at[f]))
        fetch[f].start()
    for f in range(FIELDS):
        fetch[f].wait()
        line = held[f].reshape(NZ, 16 * 128)
        out = jnp.dot(op_ref[...], line, preferred_element_type=F32).astype(BF)
        made[f] = out.reshape(16, CZ, 16, 128)
        send[f].start()
    for copy in send:
        copy.wait()


def line_z(lines, deriv_t):
    tile = pltpu.VMEM((FIELDS, 16, CZ, 16, 128), BF)
    return pl.pallas_call(
        line_z_kernel,
        in_specs=[pl.BlockSpec(memory_space=pl.ANY), pl.BlockSpec(memory_space=pltpu.VMEM)],
        out_specs=pl.BlockSpec(memory_space=pl.ANY),
        out_shape=hbm_out(lines.shape, BF),
        scratch_shapes=[
            tile,
            tile,
            pltpu.SemaphoreType.DMA((FIELDS,)),
            pltpu.SemaphoreType.DMA((FIELDS,)),
        ],
        compiler_params=params(),
        cost_estimate=cost(2 * lines.size * NZ, 4 * lines.size),
        name="line_z",
    )(in_vmem(lines), deriv_t)


def update(before, state, metric, alongs, directions=(0, 1, 2)):
    recip = 1.0 / state[0]
    vel = [state[1 + i] * recip for i in range(3)]
    speed_sq = vel[0] * vel[0] + vel[1] * vel[1] + vel[2] * vel[2]
    enthalpy = (1.0 + gamma_less) * (state[4] * recip) - 0.5 * gamma_less * speed_sq
    press = energy = back = None
    mom = [None] * 3
    plus = lambda a, b: b if a is None else a + b
    for d in directions:
        weight, along = metric[d], alongs[d]
        weighted_vel = weight * vel[d]
        turn = weight * (
            along[4] * enthalpy + along[1] * vel[0] + along[2] * vel[1] + along[3] * vel[2]
        )
        back = plus(back, turn * vel[d])
        mom[d] = plus(mom[d], weight * along[0] + turn)
        for m in range(3):
            mom[m] = plus(mom[m], weighted_vel * along[1 + m])
        work = weighted_vel * along[4]
        energy = plus(energy, work)
        press = plus(press, weight * along[1 + d] + work)
    press = gamma_less * press
    pulled = [0.5 * speed_sq * press - back]
    pulled += [mom[m] - vel[m] * press for m in range(3)]
    pulled += [energy + press]
    return [before[f] - section_step * pulled[f] for f in range(5)]


def chunks(body):
    def step(n, carry):
        z, a = n // 4, n % 4
        rows = pl.ds(pl.multiple_of(a * 16, 16), 16)
        for b in range(4):
            body(z, a * 4 + b, rows, slice(128 * b, 128 * b + 128))
        return carry

    lax.fori_loop(0, PLANES * 4, step, 0)


def update_xy_kernel(adj_ref, state_ref, metric_ref, op_ref, y_ref, out_ref, along_x):
    for f in range(FIELDS):
        along_x[f] = jnp.dot(
            adj_ref[f].reshape(PLANES * CY, NX), op_ref[...], preferred_element_type=F32
        ).reshape(PLANES, CY, NX)

    def body(z, piece, rows, cols):
        load = lambda ref, n: [ref[f, z, rows, cols].astype(F32) for f in range(n)]
        alongs = [
            [along_x[f, z, rows, cols] for f in range(5)],
            [y_ref[z // 2, f, z % 2, rows, cols].astype(F32) for f in range(5)],
        ]
        new = update(load(adj_ref, 5), load(state_ref, 5), load(metric_ref, 2), alongs, (0, 1))
        for f in range(5):
            out_ref[f, z, rows, cols] = new[f]

    chunks(body)


def update_xy(adjoint, state, metric, deriv_x, along_y):
    plane = lambda n: pl.BlockSpec((n, PLANES, CY, NX), lambda i: (0, i, 0, 0))
    cells = CZ * CY * NX
    return pl.pallas_call(
        update_xy_kernel,
        grid=(CZ // PLANES,),
        in_specs=[
            plane(5),
            plane(5),
            plane(2),
            pl.BlockSpec((NX, NX), lambda i: (0, 0)),
            pl.BlockSpec((PLANES // 2, 5, 2, CY, NX), lambda i: (i, 0, 0, 0, 0)),
        ],
        out_specs=plane(5),
        out_shape=hbm_out(adjoint.shape, F32),
        scratch_shapes=[pltpu.VMEM((FIELDS, PLANES, CY, NX), F32)],
        compiler_params=params(),
        cost_estimate=cost(cells * 2 * 5 * NX + cells * 10000, cells * 54),
        name="update_xy",
    )(*in_hbm(adjoint, state, metric, deriv_x, along_y))


def update_z_kernel(before_ref, state_ref, metric_ref, z_ref, after_ref, out_ref):
    def body(z, piece, rows, cols):
        before = [before_ref[f, z, rows, cols] for f in range(5)]
        state = [state_ref[f, z, rows, cols].astype(F32) for f in range(5)]
        metric = {2: metric_ref[0, z, rows, cols].astype(F32)}
        along = {2: [z_ref[piece, f, z].astype(F32) for f in range(5)]}
        new = update(before, state, metric, along, (2,))
        for f in range(5):
            out_ref[f, z, rows, cols] = new[f].astype(BF)

    chunks(body)


def update_z(before, state, metric, along_z, after):
    plane = lambda n: pl.BlockSpec((n, PLANES, CY, NX), lambda i: (0, i, 0, 0))
    cells = CZ * CY * NX
    return pl.pallas_call(
        update_z_kernel,
        grid=(CZ // PLANES,),
        in_specs=[
            plane(5),
            plane(5),
            pl.BlockSpec((1, PLANES, CY, NX), lambda i: (2, i, 0, 0)),
            pl.BlockSpec((16, 5, PLANES, 16, 128), lambda i: (0, 0, i, 0, 0)),
            pl.BlockSpec(memory_space=pl.ANY),
        ],
        out_specs=plane(5),
        out_shape=jax.ShapeDtypeStruct(state.shape, BF),
        compiler_params=params(),
        cost_estimate=cost(cells * 10000, cells * 52),
        name="update_z",
    )(*in_hbm(before, state, metric), in_vmem(along_z), after)


def pick_rows(onehot_ref, row, f):
    @pl.when(f == 0)
    def _():
        count = onehot_ref.shape[1]
        at = lax.broadcasted_iota(jnp.int32, (CELLS, count), 1)
        onehot_ref[...] = jnp.where(at == row, 1.0, 0.0).astype(BF)

    return onehot_ref[...]


def pick_lane(rows, lane):
    at = lax.broadcasted_iota(jnp.int32, rows.shape, 1)
    return jnp.sum(jnp.where(at == lane, rows, 0.0), axis=1, keepdims=True)


def keep(held, value, f):
    lane = lax.broadcasted_iota(jnp.int32, (CELLS, 128), 1)
    held[...] = jnp.where(lane == f, value, held[...])


def pick_kernel(cell_ref, field_ref, out_ref, onehot_ref, held):
    f = pl.program_id(0)
    cell = cell_ref[:, 0:1]
    onehot = pick_rows(onehot_ref, cell // NX, f)

    @pl.when(f == 0)
    def _():
        held[...] = jnp.zeros_like(held)

    rows = jnp.dot(onehot, field_ref[...].reshape(CZ * CY, NX), preferred_element_type=F32)
    keep(held, pick_lane(rows, cell % NX), f)

    @pl.when(f == pl.num_programs(0) - 1)
    def _():
        out_ref[...] = held[...].T[0:8]


def pick_cells(cells, fields, spec, count):
    return pl.pallas_call(
        pick_kernel,
        grid=(count,),
        in_specs=[pl.BlockSpec((CELLS, 128), lambda f: (0, 0)), spec],
        out_specs=pl.BlockSpec((8, CELLS), lambda f: (0, 0)),
        out_shape=jax.ShapeDtypeStruct((8, CELLS), F32),
        scratch_shapes=[pltpu.VMEM((CELLS, CZ * CY), BF), pltpu.VMEM((CELLS, 128), F32)],
        compiler_params=params(),
        cost_estimate=cost(2 * count * CELLS * CZ * CY * NX, count * CZ * CY * NX * 2),
        name="pick_cells",
    )(cells, *in_hbm(fields))


def pick_x_kernel(cell_ref, field_ref, op_ref, adj_out, along_out, onehot_ref, column, held, along):
    f = pl.program_id(0)
    cell = cell_ref[:, 0:1]
    x = cell % NX
    onehot = pick_rows(onehot_ref, cell // NX, f)

    @pl.when(f == 0)
    def _():
        at = lax.broadcasted_iota(jnp.int32, (CELLS, NX), 1)
        pick_x = jnp.where(at == x, 1.0, 0.0).astype(BF)
        column[...] = jnp.dot(pick_x, op_ref[...], preferred_element_type=F32)
        held[...] = jnp.zeros_like(held)
        along[...] = jnp.zeros_like(along)

    rows = jnp.dot(onehot, field_ref[...].reshape(CZ * CY, NX), preferred_element_type=F32)
    keep(held, pick_lane(rows, x), f)
    keep(along, jnp.sum(rows * column[...], axis=1, keepdims=True), f)

    @pl.when(f == pl.num_programs(0) - 1)
    def _():
        adj_out[...] = held[...].T[0:8]
        along_out[...] = along[...].T[0:8]


def pick_x(cells, adjoint, deriv_t):
    return pl.pallas_call(
        pick_x_kernel,
        grid=(FIELDS,),
        in_specs=[
            pl.BlockSpec((CELLS, 128), lambda f: (0, 0)),
            pl.BlockSpec((1, CZ, CY, NX), lambda f: (f, 0, 0, 0)),
            pl.BlockSpec((NX, NX), lambda f: (0, 0)),
        ],
        out_specs=[pl.BlockSpec((8, CELLS), lambda f: (0, 0))] * 2,
        out_shape=[jax.ShapeDtypeStruct((8, CELLS), F32)] * 2,
        scratch_shapes=[
            pltpu.VMEM((CELLS, CZ * CY), BF),
            pltpu.VMEM((CELLS, NX), F32),
            pltpu.VMEM((CELLS, 128), F32),
            pltpu.VMEM((CELLS, 128), F32),
        ],
        compiler_params=params(),
        cost_estimate=cost(2 * 5 * CELLS * CZ * CY * NX, 5 * CZ * CY * NX * 2),
        name="pick_x",
    )(cells, *in_hbm(adjoint), deriv_t)


def surface_kernel(
    cell_ref, z_ref, adj_ref, x_ref, y_ref, state_ref, metric_ref, normal_ref, basis_ref,
    out_ref, onehot, total,
):
    cell = cell_ref[:, 0:1]
    x, y, z = cell % NX, cell // NX % CY, cell // (NX * CY)
    row = ((y // 16 * 4 + x // 128) * CZ + z) * 16 + y % 16
    for n in range(4):
        at = lax.broadcasted_iota(jnp.int32, (CELLS, 1024), 1) + 1024 * n
        onehot[:, 1024 * n : 1024 * (n + 1)] = jnp.where(at == row, 1.0, 0.0).astype(BF)
    fields = [z_ref[:, f].reshape(4096, 128) for f in range(FIELDS)]
    total[...] = jnp.dot(
        onehot[...], jnp.concatenate(fields, axis=1), preferred_element_type=F32
    )
    lane = lax.broadcasted_iota(jnp.int32, (CELLS, 128), 1)
    here = lane == x % 128
    held = jnp.zeros((CELLS, 128), F32)
    for f in range(FIELDS):
        value = jnp.where(here, total[:, 128 * f : 128 * (f + 1)], 0.0)
        held = jnp.where(lane == f, jnp.sum(value, axis=1, keepdims=True), held)
    lines = lambda ref, n: [ref[i : i + 1, :] for i in range(n)]
    picked = held.T
    along_z = [picked[i : i + 1, :] for i in range(5)]
    state = lines(state_ref, 5)
    new = update(
        lines(adj_ref, 5), state, lines(metric_ref, 3),
        [lines(x_ref, 5), lines(y_ref, 5), along_z],
    )
    work = sum(state[1 + i] * (state[1 + i] / state[0]) for i in range(3))
    press = gamma_less * (state[4] - 0.5 * work)
    normal = lines(normal_ref, 3)
    force = sum(normal[i] * new[1 + i].astype(BF).astype(F32) for i in range(3))
    sens = jnp.broadcast_to((press * force).astype(BF), (16, CELLS))
    terms = jnp.dot(sens, basis_ref[...], preferred_element_type=F32)[0:1]
    out_ref[...] = jnp.broadcast_to(terms.reshape(1, 1, 256), out_ref.shape)


def surface_terms(cells, along_z, adj, along_x, along_y, state, metric, normals, basis):
    vmem = pl.BlockSpec(memory_space=pltpu.VMEM)
    return pl.pallas_call(
        surface_kernel,
        in_specs=[vmem] * 9,
        out_specs=vmem,
        out_shape=jax.ShapeDtypeStruct((128, 1, 256), F32),
        scratch_shapes=[
            pltpu.VMEM((CELLS, 4096), BF),
            pltpu.VMEM((CELLS, FIELDS * 128), F32),
        ],
        compiler_params=params(),
        cost_estimate=cost(2 * 5 * CELLS * CZ * CY * NX, 5 * CZ * CY * NX * 2),
        name="surface_terms",
    )(cells, in_vmem(along_z), adj, along_x, along_y, state, metric, normals, basis)


def normalized_kernel(terms_ref, out_ref):
    summed = jnp.sum(terms_ref[...], axis=0)
    mean = jnp.sum(summed * summed, axis=1, keepdims=True) * (1.0 / 256)
    out_ref[...] = summed / jnp.sqrt(mean + 1e-06)


def normalized(terms):
    return pl.pallas_call(
        normalized_kernel,
        out_shape=jax.ShapeDtypeStruct((1, 256), F32),
        cost_estimate=cost(4 * terms.size, 4 * terms.size),
        name="normalized",
    )(in_vmem(terms))


def on_device(
    adjoint, state, metric, deriv_x, deriv_y, deriv_z, surf_cells, surf_normal, shape_basis
):
    to_y, to_z = pieces(adjoint)
    lines_y = lax.all_to_all(to_y, "py", 0, 0)

    operators = (deriv_x, deriv_y, deriv_z)
    (deriv_x, deriv_y, deriv_z), surf_cells, surf_normal, to_z, lines_y = lax.optimization_barrier(
        (operators, surf_cells, surf_normal, to_z, lines_y)
    )
    lines_z = lax.all_to_all(to_z, "pz", 0, 0)
    products_y = line_y(lines_y, deriv_y.T)
    cells = jnp.broadcast_to(surf_cells.reshape(CELLS, 1), (CELLS, 128))
    normals = jnp.transpose(surf_normal, (1, 0, 2)).reshape(3, CELLS).astype(F32)
    normals = jnp.pad(normals, ((0, 5), (0, 0)))
    plain = pl.BlockSpec((1, CZ, CY, NX), lambda f: (f, 0, 0, 0))
    picked_state = pick_cells(cells, state, plain, 5)
    picked_metric = pick_cells(cells, metric, plain, 3)
    picked_adj, picked_x = pick_x(cells, adjoint, deriv_x.T)
    picked = (picked_adj, picked_x, picked_state, picked_metric)
    products_y, lines_z, cells, normals, picked, deriv_zt = lax.optimization_barrier(
        (products_y, lines_z, cells, normals, picked, deriv_z.T)
    )
    picked_adj, picked_x, picked_state, picked_metric = picked

    back_y = lax.all_to_all(products_y, "py", 0, 0)
    lines_z, back_y, cells, deriv_x = lax.optimization_barrier((lines_z, back_y, cells, deriv_x))
    back_z = lax.all_to_all(line_z(lines_z, deriv_zt), "pz", 0, 0)

    lines = pl.BlockSpec((8, 1, 2, CY, NX), lambda f: (0, f, 0, 0, 0))
    picked_y = pick_cells(cells, back_y, lines, 5)
    before = update_xy(adjoint, state, metric, deriv_x, back_y)
    back_z, before, picked_y = lax.optimization_barrier((back_z, before, picked_y))
    terms = surface_terms(
        cells, back_z, picked_adj, picked_x, picked_y, picked_state, picked_metric, normals,
        shape_basis,
    )
    result = update_z(before, state, metric, back_z, terms)
    all_terms = lax.all_to_all(terms, ("py", "pz"), 0, 0)
    return (result, normalized(all_terms)[0])


def solution(mesh):
    return jax.shard_map(
        on_device,
        mesh=mesh,
        in_specs=(
            P(None, "pz", "py", None),
            P(None, "pz", "py", None),
            P(None, "pz", "py", None),
            P(),
            P(),
            P(),
            P(("py", "pz"), None),
            P(("py", "pz"), None, None),
            P(("py", "pz"), None),
        ),
        out_specs=(P(None, "pz", "py", None), P()),
        check_vma=False,
    )
```

```python
import jax
import jax.numpy as jnp
from jax import lax
from jax.experimental import pallas as pl
from jax.experimental.pallas import tpu as pltpu
from jax.sharding import PartitionSpec as P

gamma_less = 0.4
section_step = 0.5
FIELDS, CZ, CY, NX, NZ = 5, 16, 64, 512, 256
CELLS = 512
PLANES = 4
BF, F32 = jnp.bfloat16, jnp.float32
MIB = 1024 * 1024


def params(mib=24):
    return pltpu.CompilerParams(vmem_limit_bytes=mib * MIB)


def in_hbm(*arrays):
    return [pltpu.with_memory_space_constraint(array, pltpu.HBM) for array in arrays]


def in_vmem(array):
    return pltpu.with_memory_space_constraint(array, pltpu.VMEM)


def hbm_out(shape, dtype):
    return pltpu.HBM(shape, dtype)


def cost(flops, nbytes):
    return pl.CostEstimate(flops=int(flops), bytes_accessed=int(nbytes), transcendentals=0)


def line_y_kernel(in_ref, op_ref, out_ref):
    line = in_ref[...].reshape(512, NX)
    out = jnp.dot(op_ref[...], line, preferred_element_type=F32)
    out_ref[...] = out.astype(BF).reshape(out_ref.shape)


def line_y(lines, deriv_t):
    n, f, z = lines.shape[:3]
    spec = pl.BlockSpec((n, 1, 1, CY, NX), lambda i, j: (0, i, j, 0, 0))
    return pl.pallas_call(
        line_y_kernel,
        grid=(f, z),
        in_specs=[spec, pl.BlockSpec((512, 512), lambda i, j: (0, 0))],
        out_specs=spec,
        out_shape=hbm_out(lines.shape, BF),
        compiler_params=params(),
        cost_estimate=cost(2 * lines.size * 512, 4 * lines.size),
        name="line_y",
    )(*in_hbm(lines), deriv_t)


def pieces_kernel(in_ref, y_ref, z_ref, sem):
    fetch = []
    for f in range(FIELDS):
        for i in range(8):
            planes = in_ref.at[f, pl.ds(2 * i, 2)]
            fetch.append(pltpu.make_async_copy(planes, y_ref.at[i, f], sem.at[8 * f + i]))
            fetch[-1].start()
    for f in range(FIELDS):
        for i in range(8):
            fetch[8 * f + i].wait()
            for a in range(4):
                for b in range(4):
                    part = y_ref[i, f, :, 16 * a : 16 * a + 16, 128 * b : 128 * b + 128]
                    z_ref[4 * a + b, f, 2 * i : 2 * i + 2] = part


def pieces(adjoint):
    vmem = pl.BlockSpec(memory_space=pltpu.VMEM)
    return pl.pallas_call(
        pieces_kernel,
        in_specs=[pl.BlockSpec(memory_space=pl.ANY)],
        out_specs=[vmem, vmem],
        out_shape=[
            pltpu.VMEM((8, FIELDS, 2, CY, NX), BF),
            pltpu.VMEM((16, FIELDS, CZ, 16, 128), BF),
        ],
        scratch_shapes=[pltpu.SemaphoreType.DMA((FIELDS * 8,))],
        compiler_params=params(),
        cost_estimate=cost(adjoint.size, 6 * adjoint.size),
        name="pieces",
    )(*in_hbm(adjoint))


def line_z_kernel(in_ref, op_ref, out_ref, held, made, in_sem, out_sem):
    fetch, send = [], []
    for f in range(FIELDS):
        fetch.append(pltpu.make_async_copy(in_ref.at[:, f], held.at[f], in_sem.at[f]))
        send.append(pltpu.make_async_copy(made.at[f], out_ref.at[:, f], out_sem.at[f]))
        fetch[f].start()
    for f in range(FIELDS):
        fetch[f].wait()
        line = held[f].reshape(NZ, 16 * 128)
        out = jnp.dot(op_ref[...], line, preferred_element_type=F32).astype(BF)
        made[f] = out.reshape(16, CZ, 16, 128)
        send[f].start()
    for copy in send:
        copy.wait()


def line_z(lines, deriv_t):
    tile = pltpu.VMEM((FIELDS, 16, CZ, 16, 128), BF)
    return pl.pallas_call(
        line_z_kernel,
        in_specs=[pl.BlockSpec(memory_space=pl.ANY), pl.BlockSpec(memory_space=pltpu.VMEM)],
        out_specs=pl.BlockSpec(memory_space=pl.ANY),
        out_shape=hbm_out(lines.shape, BF),
        scratch_shapes=[
            tile,
            tile,
            pltpu.SemaphoreType.DMA((FIELDS,)),
            pltpu.SemaphoreType.DMA((FIELDS,)),
        ],
        compiler_params=params(),
        cost_estimate=cost(2 * lines.size * NZ, 4 * lines.size),
        name="line_z",
    )(in_vmem(lines), deriv_t)


def update(before, state, metric, alongs, directions=(0, 1, 2)):
    recip = 1.0 / state[0]
    vel = [state[1 + i] * recip for i in range(3)]
    speed_sq = vel[0] * vel[0] + vel[1] * vel[1] + vel[2] * vel[2]
    enthalpy = (1.0 + gamma_less) * (state[4] * recip) - 0.5 * gamma_less * speed_sq
    press = energy = back = None
    mom = [None] * 3
    plus = lambda a, b: b if a is None else a + b
    for d in directions:
        weight, along = metric[d], alongs[d]
        weighted_vel = weight * vel[d]
        turn = weight * (
            along[4] * enthalpy + along[1] * vel[0] + along[2] * vel[1] + along[3] * vel[2]
        )
        back = plus(back, turn * vel[d])
        mom[d] = plus(mom[d], weight * along[0] + turn)
        for m in range(3):
            mom[m] = plus(mom[m], weighted_vel * along[1 + m])
        work = weighted_vel * along[4]
        energy = plus(energy, work)
        press = plus(press, weight * along[1 + d] + work)
    press = gamma_less * press
    pulled = [0.5 * speed_sq * press - back]
    pulled += [mom[m] - vel[m] * press for m in range(3)]
    pulled += [energy + press]
    return [before[f] - section_step * pulled[f] for f in range(5)]


def chunks(body):
    def step(n, carry):
        z, a = n // 4, n % 4
        rows = pl.ds(pl.multiple_of(a * 16, 16), 16)
        for b in range(4):
            body(z, a * 4 + b, rows, slice(128 * b, 128 * b + 128))
        return carry

    lax.fori_loop(0, PLANES * 4, step, 0)


def update_xy_kernel(adj_ref, state_ref, metric_ref, op_ref, y_ref, out_ref, along_x):
    for f in range(FIELDS):
        along_x[f] = jnp.dot(
            adj_ref[f].reshape(PLANES * CY, NX), op_ref[...], preferred_element_type=F32
        ).reshape(PLANES, CY, NX)

    def body(z, piece, rows, cols):
        load = lambda ref, n: [ref[f, z, rows, cols].astype(F32) for f in range(n)]
        alongs = [
            [along_x[f, z, rows, cols] for f in range(5)],
            [y_ref[z // 2, f, z % 2, rows, cols].astype(F32) for f in range(5)],
        ]
        new = update(load(adj_ref, 5), load(state_ref, 5), load(metric_ref, 2), alongs, (0, 1))
        for f in range(5):
            out_ref[f, z, rows, cols] = new[f].astype(BF)

    chunks(body)


def update_xy(adjoint, state, metric, deriv_x, along_y):
    plane = lambda n: pl.BlockSpec((n, PLANES, CY, NX), lambda i: (0, i, 0, 0))
    cells = CZ * CY * NX
    return pl.pallas_call(
        update_xy_kernel,
        grid=(CZ // PLANES,),
        in_specs=[
            plane(5),
            plane(5),
            plane(2),
            pl.BlockSpec((NX, NX), lambda i: (0, 0)),
            pl.BlockSpec((PLANES // 2, 5, 2, CY, NX), lambda i: (i, 0, 0, 0, 0)),
        ],
        out_specs=plane(5),
        out_shape=hbm_out(adjoint.shape, BF),
        scratch_shapes=[pltpu.VMEM((FIELDS, PLANES, CY, NX), F32)],
        compiler_params=params(),
        cost_estimate=cost(cells * 2 * 5 * NX + cells * 10000, cells * 54),
        name="update_xy",
    )(*in_hbm(adjoint, state, metric, deriv_x, along_y))


def update_z_kernel(before_ref, state_ref, metric_ref, z_ref, after_ref, out_ref):
    def body(z, piece, rows, cols):
        before = [before_ref[f, z, rows, cols].astype(F32) for f in range(5)]
        state = [state_ref[f, z, rows, cols].astype(F32) for f in range(5)]
        metric = {2: metric_ref[0, z, rows, cols].astype(F32)}
        along = {2: [z_ref[piece, f, z].astype(F32) for f in range(5)]}
        new = update(before, state, metric, along, (2,))
        for f in range(5):
            out_ref[f, z, rows, cols] = new[f].astype(BF)

    chunks(body)


def update_z(before, state, metric, along_z, after):
    plane = lambda n: pl.BlockSpec((n, PLANES, CY, NX), lambda i: (0, i, 0, 0))
    cells = CZ * CY * NX
    return pl.pallas_call(
        update_z_kernel,
        grid=(CZ // PLANES,),
        in_specs=[
            plane(5),
            plane(5),
            pl.BlockSpec((1, PLANES, CY, NX), lambda i: (2, i, 0, 0)),
            pl.BlockSpec((16, 5, PLANES, 16, 128), lambda i: (0, 0, i, 0, 0)),
            pl.BlockSpec(memory_space=pl.ANY),
        ],
        out_specs=plane(5),
        out_shape=jax.ShapeDtypeStruct(state.shape, BF),
        compiler_params=params(),
        cost_estimate=cost(cells * 10000, cells * 52),
        name="update_z",
    )(*in_hbm(before, state, metric), *in_hbm(along_z), after)


def pick_rows(onehot_ref, row, f):
    @pl.when(f == 0)
    def _():
        count = onehot_ref.shape[1]
        at = lax.broadcasted_iota(jnp.int32, (CELLS, count), 1)
        onehot_ref[...] = jnp.where(at == row, 1.0, 0.0).astype(BF)

    return onehot_ref[...]


def pick_lane(rows, lane):
    at = lax.broadcasted_iota(jnp.int32, rows.shape, 1)
    return jnp.sum(jnp.where(at == lane, rows, 0.0), axis=1, keepdims=True)


def keep(held, value, f):
    lane = lax.broadcasted_iota(jnp.int32, (CELLS, 128), 1)
    held[...] = jnp.where(lane == f, value, held[...])


def pick_kernel(cell_ref, field_ref, out_ref, onehot_ref, held):
    f = pl.program_id(0)
    cell = cell_ref[:, 0:1]
    onehot = pick_rows(onehot_ref, cell // NX, f)

    @pl.when(f == 0)
    def _():
        held[...] = jnp.zeros_like(held)

    rows = jnp.dot(onehot, field_ref[...].reshape(CZ * CY, NX), preferred_element_type=F32)
    keep(held, pick_lane(rows, cell % NX), f)

    @pl.when(f == pl.num_programs(0) - 1)
    def _():
        out_ref[...] = held[...].T[0:8]


def pick_cells(cells, fields, spec, count):
    return pl.pallas_call(
        pick_kernel,
        grid=(count,),
        in_specs=[pl.BlockSpec((CELLS, 128), lambda f: (0, 0)), spec],
        out_specs=pl.BlockSpec((8, CELLS), lambda f: (0, 0)),
        out_shape=jax.ShapeDtypeStruct((8, CELLS), F32),
        scratch_shapes=[pltpu.VMEM((CELLS, CZ * CY), BF), pltpu.VMEM((CELLS, 128), F32)],
        compiler_params=params(),
        cost_estimate=cost(2 * count * CELLS * CZ * CY * NX, count * CZ * CY * NX * 2),
        name="pick_cells",
    )(cells, *in_hbm(fields))


def pick_x_kernel(cell_ref, field_ref, op_ref, adj_out, along_out, onehot_ref, column, held, along):
    f = pl.program_id(0)
    cell = cell_ref[:, 0:1]
    x = cell % NX
    onehot = pick_rows(onehot_ref, cell // NX, f)

    @pl.when(f == 0)
    def _():
        at = lax.broadcasted_iota(jnp.int32, (CELLS, NX), 1)
        pick_x = jnp.where(at == x, 1.0, 0.0).astype(BF)
        column[...] = jnp.dot(pick_x, op_ref[...], preferred_element_type=F32)
        held[...] = jnp.zeros_like(held)
        along[...] = jnp.zeros_like(along)

    rows = jnp.dot(onehot, field_ref[...].reshape(CZ * CY, NX), preferred_element_type=F32)
    keep(held, pick_lane(rows, x), f)
    keep(along, jnp.sum(rows * column[...], axis=1, keepdims=True), f)

    @pl.when(f == pl.num_programs(0) - 1)
    def _():
        adj_out[...] = held[...].T[0:8]
        along_out[...] = along[...].T[0:8]


def pick_x(cells, adjoint, deriv_t):
    return pl.pallas_call(
        pick_x_kernel,
        grid=(FIELDS,),
        in_specs=[
            pl.BlockSpec((CELLS, 128), lambda f: (0, 0)),
            pl.BlockSpec((1, CZ, CY, NX), lambda f: (f, 0, 0, 0)),
            pl.BlockSpec((NX, NX), lambda f: (0, 0)),
        ],
        out_specs=[pl.BlockSpec((8, CELLS), lambda f: (0, 0))] * 2,
        out_shape=[jax.ShapeDtypeStruct((8, CELLS), F32)] * 2,
        scratch_shapes=[
            pltpu.VMEM((CELLS, CZ * CY), BF),
            pltpu.VMEM((CELLS, NX), F32),
            pltpu.VMEM((CELLS, 128), F32),
            pltpu.VMEM((CELLS, 128), F32),
        ],
        compiler_params=params(),
        cost_estimate=cost(2 * 5 * CELLS * CZ * CY * NX, 5 * CZ * CY * NX * 2),
        name="pick_x",
    )(cells, *in_hbm(adjoint), deriv_t)


def surface_kernel(
    cell_ref, z_ref, adj_ref, x_ref, y_ref, state_ref, metric_ref, normal_ref, basis_ref,
    out_ref, onehot, total, pieces_z, sem,
):
    fetch = pltpu.make_async_copy(z_ref, pieces_z, sem)
    fetch.start()
    cell = cell_ref[:, 0:1]
    x, y, z = cell % NX, cell // NX % CY, cell // (NX * CY)
    row = ((y // 16 * 4 + x // 128) * CZ + z) * 16 + y % 16
    for n in range(4):
        at = lax.broadcasted_iota(jnp.int32, (CELLS, 1024), 1) + 1024 * n
        onehot[:, 1024 * n : 1024 * (n + 1)] = jnp.where(at == row, 1.0, 0.0).astype(BF)
    fetch.wait()
    fields = [pieces_z[:, f].reshape(4096, 128) for f in range(FIELDS)]
    total[...] = jnp.dot(
        onehot[...], jnp.concatenate(fields, axis=1), preferred_element_type=F32
    )
    lane = lax.broadcasted_iota(jnp.int32, (CELLS, 128), 1)
    here = lane == x % 128
    held = jnp.zeros((CELLS, 128), F32)
    for f in range(FIELDS):
        value = jnp.where(here, total[:, 128 * f : 128 * (f + 1)], 0.0)
        held = jnp.where(lane == f, jnp.sum(value, axis=1, keepdims=True), held)
    lines = lambda ref, n: [ref[i : i + 1, :] for i in range(n)]
    picked = held.T
    along_z = [picked[i : i + 1, :] for i in range(5)]
    state = lines(state_ref, 5)
    new = update(
        lines(adj_ref, 5), state, lines(metric_ref, 3),
        [lines(x_ref, 5), lines(y_ref, 5), along_z],
    )
    work = sum(state[1 + i] * (state[1 + i] / state[0]) for i in range(3))
    press = gamma_less * (state[4] - 0.5 * work)
    normal = lines(normal_ref, 3)
    force = sum(normal[i] * new[1 + i].astype(BF).astype(F32) for i in range(3))
    sens = jnp.broadcast_to((press * force).astype(BF), (16, CELLS))
    terms = jnp.dot(sens, basis_ref[...], preferred_element_type=F32)[0:1]
    out_ref[...] = jnp.broadcast_to(terms.reshape(1, 1, 256), out_ref.shape)


def surface_terms(cells, along_z, adj, along_x, along_y, state, metric, normals, basis):
    vmem = pl.BlockSpec(memory_space=pltpu.VMEM)
    return pl.pallas_call(
        surface_kernel,
        in_specs=[vmem, pl.BlockSpec(memory_space=pl.ANY)] + [vmem] * 7,
        out_specs=vmem,
        out_shape=jax.ShapeDtypeStruct((128, 1, 256), F32),
        scratch_shapes=[
            pltpu.VMEM((CELLS, 4096), BF),
            pltpu.VMEM((CELLS, FIELDS * 128), F32),
            pltpu.VMEM((16, FIELDS, CZ, 16, 128), BF),
            pltpu.SemaphoreType.DMA,
        ],
        compiler_params=params(),
        cost_estimate=cost(2 * 5 * CELLS * CZ * CY * NX, 5 * CZ * CY * NX * 2),
        name="surface_terms",
    )(cells, *in_hbm(along_z), adj, along_x, along_y, state, metric, normals, basis)


def normalized_kernel(terms_ref, out_ref):
    summed = jnp.sum(terms_ref[...], axis=0)
    mean = jnp.sum(summed * summed, axis=1, keepdims=True) * (1.0 / 256)
    out_ref[...] = summed / jnp.sqrt(mean + 1e-06)


def normalized(terms):
    return pl.pallas_call(
        normalized_kernel,
        out_shape=jax.ShapeDtypeStruct((1, 256), F32),
        cost_estimate=cost(4 * terms.size, 4 * terms.size),
        name="normalized",
    )(in_vmem(terms))


def on_device(
    adjoint, state, metric, deriv_x, deriv_y, deriv_z, surf_cells, surf_normal, shape_basis
):
    to_y, to_z = pieces(adjoint)
    lines_y = lax.all_to_all(to_y, "py", 0, 0)

    operators = (deriv_x, deriv_y, deriv_z)
    (deriv_x, deriv_y, deriv_z), surf_cells, surf_normal, to_z, lines_y = lax.optimization_barrier(
        (operators, surf_cells, surf_normal, to_z, lines_y)
    )
    lines_z = lax.all_to_all(to_z, "pz", 0, 0)
    products_y = line_y(lines_y, deriv_y.T)
    cells = jnp.broadcast_to(surf_cells.reshape(CELLS, 1), (CELLS, 128))
    normals = jnp.transpose(surf_normal, (1, 0, 2)).reshape(3, CELLS).astype(F32)
    normals = jnp.pad(normals, ((0, 5), (0, 0)))
    plain = pl.BlockSpec((1, CZ, CY, NX), lambda f: (f, 0, 0, 0))
    picked_state = pick_cells(cells, state, plain, 5)
    picked_metric = pick_cells(cells, metric, plain, 3)
    picked_adj, picked_x = pick_x(cells, adjoint, deriv_x.T)
    picked = (picked_adj, picked_x, picked_state, picked_metric)
    products_y, lines_z, cells, normals, picked, deriv_zt = lax.optimization_barrier(
        (products_y, lines_z, cells, normals, picked, deriv_z.T)
    )
    picked_adj, picked_x, picked_state, picked_metric = picked

    back_y = lax.all_to_all(products_y, "py", 0, 0)
    lines_z, back_y, cells, deriv_x = lax.optimization_barrier((lines_z, back_y, cells, deriv_x))
    back_z = lax.all_to_all(line_z(lines_z, deriv_zt), "pz", 0, 0)

    lines = pl.BlockSpec((8, 1, 2, CY, NX), lambda f: (0, f, 0, 0, 0))
    picked_y = pick_cells(cells, back_y, lines, 5)
    before = update_xy(adjoint, state, metric, deriv_x, back_y)
    back_z, before, picked_y = lax.optimization_barrier((back_z, before, picked_y))
    terms = surface_terms(
        cells, back_z, picked_adj, picked_x, picked_y, picked_state, picked_metric, normals,
        shape_basis,
    )
    result = update_z(before, state, metric, back_z, terms)
    all_terms = lax.all_to_all(terms, ("py", "pz"), 0, 0)
    return (result, normalized(all_terms)[0])


def solution(mesh):
    return jax.shard_map(
        on_device,
        mesh=mesh,
        in_specs=(
            P(None, "pz", "py", None),
            P(None, "pz", "py", None),
            P(None, "pz", "py", None),
            P(),
            P(),
            P(),
            P(("py", "pz"), None),
            P(("py", "pz"), None, None),
            P(("py", "pz"), None),
        ),
        out_specs=(P(None, "pz", "py", None), P()),
        check_vma=False,
    )
```

```python
import jax
import jax.numpy as jnp
from jax import lax
from jax.experimental import pallas as pl
from jax.experimental.pallas import tpu as pltpu
from jax.sharding import PartitionSpec as P

gamma_less = 0.4
section_step = 0.5
FIELDS, CZ, CY, NX, NZ = 5, 16, 64, 512, 256
CELLS = 512
PLANES = 4
BF, F32 = jnp.bfloat16, jnp.float32
MIB = 1024 * 1024


def params(mib=24):
    return pltpu.CompilerParams(vmem_limit_bytes=mib * MIB)


def in_hbm(*arrays):
    return [pltpu.with_memory_space_constraint(array, pltpu.HBM) for array in arrays]


def in_vmem(array):
    return pltpu.with_memory_space_constraint(array, pltpu.VMEM)


def hbm_out(shape, dtype):
    return pltpu.HBM(shape, dtype)


def cost(flops, nbytes):
    return pl.CostEstimate(flops=int(flops), bytes_accessed=int(nbytes), transcendentals=0)


def line_y_kernel(in_ref, op_ref, out_ref):
    line = in_ref[...].reshape(512, NX)
    out = jnp.dot(op_ref[...], line, preferred_element_type=F32)
    out_ref[...] = out.astype(BF).reshape(out_ref.shape)


def line_y(lines, deriv_t):
    n, f, z = lines.shape[:3]
    spec = pl.BlockSpec((n, 1, 1, CY, NX), lambda i, j: (0, i, j, 0, 0))
    return pl.pallas_call(
        line_y_kernel,
        grid=(f, z),
        in_specs=[spec, pl.BlockSpec((512, 512), lambda i, j: (0, 0))],
        out_specs=spec,
        out_shape=hbm_out(lines.shape, BF),
        compiler_params=params(),
        cost_estimate=cost(2 * lines.size * 512, 4 * lines.size),
        name="line_y",
    )(*in_hbm(lines), deriv_t)


def pieces_kernel(in_ref, y_ref, z_ref, sem):
    fetch = []
    for f in range(FIELDS):
        for i in range(8):
            planes = in_ref.at[f, pl.ds(2 * i, 2)]
            fetch.append(pltpu.make_async_copy(planes, y_ref.at[i, f], sem.at[8 * f + i]))
            fetch[-1].start()
    for f in range(FIELDS):
        for i in range(8):
            fetch[8 * f + i].wait()
            for a in range(4):
                for b in range(4):
                    part = y_ref[i, f, :, 16 * a : 16 * a + 16, 128 * b : 128 * b + 128]
                    z_ref[4 * a + b, f, 2 * i : 2 * i + 2] = part


def pieces(adjoint):
    vmem = pl.BlockSpec(memory_space=pltpu.VMEM)
    return pl.pallas_call(
        pieces_kernel,
        in_specs=[pl.BlockSpec(memory_space=pl.ANY)],
        out_specs=[vmem, vmem],
        out_shape=[
            pltpu.VMEM((8, FIELDS, 2, CY, NX), BF),
            pltpu.VMEM((16, FIELDS, CZ, 16, 128), BF),
        ],
        scratch_shapes=[pltpu.SemaphoreType.DMA((FIELDS * 8,))],
        compiler_params=params(),
        cost_estimate=cost(adjoint.size, 6 * adjoint.size),
        name="pieces",
    )(*in_hbm(adjoint))


def line_z_kernel(in_ref, op_ref, out_ref, held, made, in_sem, out_sem):
    fetch, send = [], []
    for f in range(FIELDS):
        fetch.append(pltpu.make_async_copy(in_ref.at[:, f], held.at[f], in_sem.at[f]))
        send.append(pltpu.make_async_copy(made.at[f], out_ref.at[:, f], out_sem.at[f]))
    for f in range(3):
        fetch[f].start()
    for f in range(FIELDS):
        fetch[f].wait()
        if f + 3 < FIELDS:
            fetch[f + 3].start()
        line = held[f].reshape(NZ, 16 * 128)
        out = jnp.dot(op_ref[...], line, preferred_element_type=F32).astype(BF)
        made[f] = out.reshape(16, CZ, 16, 128)
        send[f].start()
    for copy in send:
        copy.wait()


def line_z(lines, deriv_t):
    tile = pltpu.VMEM((FIELDS, 16, CZ, 16, 128), BF)
    return pl.pallas_call(
        line_z_kernel,
        in_specs=[pl.BlockSpec(memory_space=pl.ANY), pl.BlockSpec(memory_space=pltpu.VMEM)],
        out_specs=pl.BlockSpec(memory_space=pl.ANY),
        out_shape=hbm_out(lines.shape, BF),
        scratch_shapes=[
            tile,
            tile,
            pltpu.SemaphoreType.DMA((FIELDS,)),
            pltpu.SemaphoreType.DMA((FIELDS,)),
        ],
        compiler_params=params(),
        cost_estimate=cost(2 * lines.size * NZ, 4 * lines.size),
        name="line_z",
    )(in_vmem(lines), deriv_t)


def update(before, state, metric, alongs, directions=(0, 1, 2)):
    recip = 1.0 / state[0]
    vel = [state[1 + i] * recip for i in range(3)]
    speed_sq = vel[0] * vel[0] + vel[1] * vel[1] + vel[2] * vel[2]
    enthalpy = (1.0 + gamma_less) * (state[4] * recip) - 0.5 * gamma_less * speed_sq
    press = energy = back = None
    mom = [None] * 3
    plus = lambda a, b: b if a is None else a + b
    for d in directions:
        weight, along = metric[d], alongs[d]
        weighted_vel = weight * vel[d]
        turn = weight * (
            along[4] * enthalpy + along[1] * vel[0] + along[2] * vel[1] + along[3] * vel[2]
        )
        back = plus(back, turn * vel[d])
        mom[d] = plus(mom[d], weight * along[0] + turn)
        for m in range(3):
            mom[m] = plus(mom[m], weighted_vel * along[1 + m])
        work = weighted_vel * along[4]
        energy = plus(energy, work)
        press = plus(press, weight * along[1 + d] + work)
    press = gamma_less * press
    pulled = [0.5 * speed_sq * press - back]
    pulled += [mom[m] - vel[m] * press for m in range(3)]
    pulled += [energy + press]
    return [before[f] - section_step * pulled[f] for f in range(5)]


def chunks(body):
    def step(n, carry):
        z, a = n // 4, n % 4
        rows = pl.ds(pl.multiple_of(a * 16, 16), 16)
        for b in range(4):
            body(z, a * 4 + b, rows, slice(128 * b, 128 * b + 128))
        return carry

    lax.fori_loop(0, PLANES * 4, step, 0)


def update_xy_kernel(adj_ref, state_ref, metric_ref, op_ref, y_ref, out_ref, along_x):
    for f in range(FIELDS):
        along_x[f] = jnp.dot(
            adj_ref[f].reshape(PLANES * CY, NX), op_ref[...], preferred_element_type=F32
        ).reshape(PLANES, CY, NX)

    def body(z, piece, rows, cols):
        load = lambda ref, n: [ref[f, z, rows, cols].astype(F32) for f in range(n)]
        alongs = [
            [along_x[f, z, rows, cols] for f in range(5)],
            [y_ref[z // 2, f, z % 2, rows, cols].astype(F32) for f in range(5)],
        ]
        new = update(load(adj_ref, 5), load(state_ref, 5), load(metric_ref, 2), alongs, (0, 1))
        for f in range(5):
            out_ref[f, z, rows, cols] = new[f]

    chunks(body)


def update_xy(adjoint, state, metric, deriv_x, along_y):
    plane = lambda n: pl.BlockSpec((n, PLANES, CY, NX), lambda i: (0, i, 0, 0))
    cells = CZ * CY * NX
    return pl.pallas_call(
        update_xy_kernel,
        grid=(CZ // PLANES,),
        in_specs=[
            plane(5),
            plane(5),
            plane(2),
            pl.BlockSpec((NX, NX), lambda i: (0, 0)),
            pl.BlockSpec((PLANES // 2, 5, 2, CY, NX), lambda i: (i, 0, 0, 0, 0)),
        ],
        out_specs=plane(5),
        out_shape=hbm_out(adjoint.shape, F32),
        scratch_shapes=[pltpu.VMEM((FIELDS, PLANES, CY, NX), F32)],
        compiler_params=params(),
        cost_estimate=cost(cells * 2 * 5 * NX + cells * 10000, cells * 54),
        name="update_xy",
    )(*in_hbm(adjoint, state, metric, deriv_x, along_y))


def update_z_kernel(before_ref, state_ref, metric_ref, z_ref, after_ref, out_ref):
    def body(z, piece, rows, cols):
        before = [before_ref[f, z, rows, cols] for f in range(5)]
        state = [state_ref[f, z, rows, cols].astype(F32) for f in range(5)]
        metric = {2: metric_ref[0, z, rows, cols].astype(F32)}
        along = {2: [z_ref[piece, f, z].astype(F32) for f in range(5)]}
        new = update(before, state, metric, along, (2,))
        for f in range(5):
            out_ref[f, z, rows, cols] = new[f].astype(BF)

    chunks(body)


def update_z(before, state, metric, along_z, after):
    plane = lambda n: pl.BlockSpec((n, PLANES, CY, NX), lambda i: (0, i, 0, 0))
    cells = CZ * CY * NX
    return pl.pallas_call(
        update_z_kernel,
        grid=(CZ // PLANES,),
        in_specs=[
            plane(5),
            plane(5),
            pl.BlockSpec((1, PLANES, CY, NX), lambda i: (2, i, 0, 0)),
            pl.BlockSpec((16, 5, PLANES, 16, 128), lambda i: (0, 0, i, 0, 0)),
            pl.BlockSpec(memory_space=pl.ANY),
        ],
        out_specs=plane(5),
        out_shape=jax.ShapeDtypeStruct(state.shape, BF),
        compiler_params=params(),
        cost_estimate=cost(cells * 10000, cells * 52),
        name="update_z",
    )(*in_hbm(before, state, metric), *in_hbm(along_z), after)


def pick_rows(onehot_ref, row, f):
    @pl.when(f == 0)
    def _():
        count = onehot_ref.shape[1]
        at = lax.broadcasted_iota(jnp.int32, (CELLS, count), 1)
        onehot_ref[...] = jnp.where(at == row, 1.0, 0.0).astype(BF)

    return onehot_ref[...]


def pick_lane(rows, lane):
    at = lax.broadcasted_iota(jnp.int32, rows.shape, 1)
    return jnp.sum(jnp.where(at == lane, rows, 0.0), axis=1, keepdims=True)


def keep(held, value, f):
    lane = lax.broadcasted_iota(jnp.int32, (CELLS, 128), 1)
    held[...] = jnp.where(lane == f, value, held[...])


def pick_kernel(cell_ref, field_ref, out_ref, onehot_ref, held):
    f = pl.program_id(0)
    cell = cell_ref[:, 0:1]
    onehot = pick_rows(onehot_ref, cell // NX, f)

    @pl.when(f == 0)
    def _():
        held[...] = jnp.zeros_like(held)

    rows = jnp.dot(onehot, field_ref[...].reshape(CZ * CY, NX), preferred_element_type=F32)
    keep(held, pick_lane(rows, cell % NX), f)

    @pl.when(f == pl.num_programs(0) - 1)
    def _():
        out_ref[...] = held[...].T[0:8]


def pick_cells(cells, fields, spec, count):
    return pl.pallas_call(
        pick_kernel,
        grid=(count,),
        in_specs=[pl.BlockSpec((CELLS, 128), lambda f: (0, 0)), spec],
        out_specs=pl.BlockSpec((8, CELLS), lambda f: (0, 0)),
        out_shape=jax.ShapeDtypeStruct((8, CELLS), F32),
        scratch_shapes=[pltpu.VMEM((CELLS, CZ * CY), BF), pltpu.VMEM((CELLS, 128), F32)],
        compiler_params=params(),
        cost_estimate=cost(2 * count * CELLS * CZ * CY * NX, count * CZ * CY * NX * 2),
        name="pick_cells",
    )(cells, *in_hbm(fields))


def pick_x_kernel(cell_ref, field_ref, op_ref, adj_out, along_out, onehot_ref, column, held, along):
    f = pl.program_id(0)
    cell = cell_ref[:, 0:1]
    x = cell % NX
    onehot = pick_rows(onehot_ref, cell // NX, f)

    @pl.when(f == 0)
    def _():
        at = lax.broadcasted_iota(jnp.int32, (CELLS, NX), 1)
        pick_x = jnp.where(at == x, 1.0, 0.0).astype(BF)
        column[...] = jnp.dot(pick_x, op_ref[...], preferred_element_type=F32)
        held[...] = jnp.zeros_like(held)
        along[...] = jnp.zeros_like(along)

    rows = jnp.dot(onehot, field_ref[...].reshape(CZ * CY, NX), preferred_element_type=F32)
    keep(held, pick_lane(rows, x), f)
    keep(along, jnp.sum(rows * column[...], axis=1, keepdims=True), f)

    @pl.when(f == pl.num_programs(0) - 1)
    def _():
        adj_out[...] = held[...].T[0:8]
        along_out[...] = along[...].T[0:8]


def pick_x(cells, adjoint, deriv_t):
    return pl.pallas_call(
        pick_x_kernel,
        grid=(FIELDS,),
        in_specs=[
            pl.BlockSpec((CELLS, 128), lambda f: (0, 0)),
            pl.BlockSpec((1, CZ, CY, NX), lambda f: (f, 0, 0, 0)),
            pl.BlockSpec((NX, NX), lambda f: (0, 0)),
        ],
        out_specs=[pl.BlockSpec((8, CELLS), lambda f: (0, 0))] * 2,
        out_shape=[jax.ShapeDtypeStruct((8, CELLS), F32)] * 2,
        scratch_shapes=[
            pltpu.VMEM((CELLS, CZ * CY), BF),
            pltpu.VMEM((CELLS, NX), F32),
            pltpu.VMEM((CELLS, 128), F32),
            pltpu.VMEM((CELLS, 128), F32),
        ],
        compiler_params=params(),
        cost_estimate=cost(2 * 5 * CELLS * CZ * CY * NX, 5 * CZ * CY * NX * 2),
        name="pick_x",
    )(cells, *in_hbm(adjoint), deriv_t)


def surface_kernel(
    cell_ref, z_ref, adj_ref, x_ref, y_ref, state_ref, metric_ref, normal_ref, basis_ref,
    out_ref, onehot, total, pieces_z, sem,
):
    fetch = pltpu.make_async_copy(z_ref, pieces_z, sem)
    fetch.start()
    cell = cell_ref[:, 0:1]
    x, y, z = cell % NX, cell // NX % CY, cell // (NX * CY)
    row = ((y // 16 * 4 + x // 128) * CZ + z) * 16 + y % 16
    for n in range(4):
        at = lax.broadcasted_iota(jnp.int32, (CELLS, 1024), 1) + 1024 * n
        onehot[:, 1024 * n : 1024 * (n + 1)] = jnp.where(at == row, 1.0, 0.0).astype(BF)
    fetch.wait()
    fields = [pieces_z[:, f].reshape(4096, 128) for f in range(FIELDS)]
    total[...] = jnp.dot(
        onehot[...], jnp.concatenate(fields, axis=1), preferred_element_type=F32
    )
    lane = lax.broadcasted_iota(jnp.int32, (CELLS, 128), 1)
    here = lane == x % 128
    held = jnp.zeros((CELLS, 128), F32)
    for f in range(FIELDS):
        value = jnp.where(here, total[:, 128 * f : 128 * (f + 1)], 0.0)
        held = jnp.where(lane == f, jnp.sum(value, axis=1, keepdims=True), held)
    lines = lambda ref, n: [ref[i : i + 1, :] for i in range(n)]
    picked = held.T
    along_z = [picked[i : i + 1, :] for i in range(5)]
    state = lines(state_ref, 5)
    new = update(
        lines(adj_ref, 5), state, lines(metric_ref, 3),
        [lines(x_ref, 5), lines(y_ref, 5), along_z],
    )
    work = sum(state[1 + i] * (state[1 + i] / state[0]) for i in range(3))
    press = gamma_less * (state[4] - 0.5 * work)
    normal = lines(normal_ref, 3)
    force = sum(normal[i] * new[1 + i].astype(BF).astype(F32) for i in range(3))
    sens = jnp.broadcast_to((press * force).astype(BF), (16, CELLS))
    terms = jnp.dot(sens, basis_ref[...], preferred_element_type=F32)[0:1]
    out_ref[...] = jnp.broadcast_to(terms.reshape(1, 1, 256), out_ref.shape)


def surface_terms(cells, along_z, adj, along_x, along_y, state, metric, normals, basis):
    vmem = pl.BlockSpec(memory_space=pltpu.VMEM)
    return pl.pallas_call(
        surface_kernel,
        in_specs=[vmem, pl.BlockSpec(memory_space=pl.ANY)] + [vmem] * 7,
        out_specs=vmem,
        out_shape=jax.ShapeDtypeStruct((128, 1, 256), F32),
        scratch_shapes=[
            pltpu.VMEM((CELLS, 4096), BF),
            pltpu.VMEM((CELLS, FIELDS * 128), F32),
            pltpu.VMEM((16, FIELDS, CZ, 16, 128), BF),
            pltpu.SemaphoreType.DMA,
        ],
        compiler_params=params(),
        cost_estimate=cost(2 * 5 * CELLS * CZ * CY * NX, 5 * CZ * CY * NX * 2),
        name="surface_terms",
    )(cells, *in_hbm(along_z), adj, along_x, along_y, state, metric, normals, basis)


def normalized_kernel(terms_ref, out_ref):
    summed = jnp.sum(terms_ref[...], axis=0)
    mean = jnp.sum(summed * summed, axis=1, keepdims=True) * (1.0 / 256)
    out_ref[...] = summed / jnp.sqrt(mean + 1e-06)


def normalized(terms):
    return pl.pallas_call(
        normalized_kernel,
        out_shape=jax.ShapeDtypeStruct((1, 256), F32),
        cost_estimate=cost(4 * terms.size, 4 * terms.size),
        name="normalized",
    )(in_vmem(terms))


def on_device(
    adjoint, state, metric, deriv_x, deriv_y, deriv_z, surf_cells, surf_normal, shape_basis
):
    to_y, to_z = pieces(adjoint)
    lines_y = lax.all_to_all(to_y, "py", 0, 0)

    operators = (deriv_x, deriv_y, deriv_z)
    (deriv_x, deriv_y, deriv_z), surf_cells, surf_normal, to_z, lines_y = lax.optimization_barrier(
        (operators, surf_cells, surf_normal, to_z, lines_y)
    )
    lines_z = lax.all_to_all(to_z, "pz", 0, 0)
    products_y = line_y(lines_y, deriv_y.T)
    cells = jnp.broadcast_to(surf_cells.reshape(CELLS, 1), (CELLS, 128))
    normals = jnp.transpose(surf_normal, (1, 0, 2)).reshape(3, CELLS).astype(F32)
    normals = jnp.pad(normals, ((0, 5), (0, 0)))
    plain = pl.BlockSpec((1, CZ, CY, NX), lambda f: (f, 0, 0, 0))
    picked_state = pick_cells(cells, state, plain, 5)
    picked_metric = pick_cells(cells, metric, plain, 3)
    picked_adj, picked_x = pick_x(cells, adjoint, deriv_x.T)
    picked = (picked_adj, picked_x, picked_state, picked_metric)
    products_y, lines_z, cells, normals, picked, deriv_zt = lax.optimization_barrier(
        (products_y, lines_z, cells, normals, picked, deriv_z.T)
    )
    picked_adj, picked_x, picked_state, picked_metric = picked

    back_y = lax.all_to_all(products_y, "py", 0, 0)
    lines_z, back_y, cells, deriv_x = lax.optimization_barrier((lines_z, back_y, cells, deriv_x))
    back_z = lax.all_to_all(line_z(lines_z, deriv_zt), "pz", 0, 0)

    lines = pl.BlockSpec((8, 1, 2, CY, NX), lambda f: (0, f, 0, 0, 0))
    picked_y = pick_cells(cells, back_y, lines, 5)
    before = update_xy(adjoint, state, metric, deriv_x, back_y)
    back_z, before, picked_y = lax.optimization_barrier((back_z, before, picked_y))
    terms = surface_terms(
        cells, back_z, picked_adj, picked_x, picked_y, picked_state, picked_metric, normals,
        shape_basis,
    )
    result = update_z(before, state, metric, back_z, terms)
    all_terms = lax.all_to_all(terms, ("py", "pz"), 0, 0)
    return (result, normalized(all_terms)[0])


def solution(mesh):
    return jax.shard_map(
        on_device,
        mesh=mesh,
        in_specs=(
            P(None, "pz", "py", None),
            P(None, "pz", "py", None),
            P(None, "pz", "py", None),
            P(),
            P(),
            P(),
            P(("py", "pz"), None),
            P(("py", "pz"), None, None),
            P(("py", "pz"), None),
        ),
        out_specs=(P(None, "pz", "py", None), P()),
        check_vma=False,
    )
```
